32 devices in a mesh: seq: 8 (over z, x), head: 4 (over y, core).
Axes of the slice: x: 2, y: 2, z: 4, core: 2. Of those that a mesh axis runs over, the one named last changes fastest.
Arguments:
- tokens: bfloat16 [4096, 2048], P('seq'), may hold values from -6 to 6
- cotangent: bfloat16 [4096, 2048], P('seq'), may hold values from -6 to 6
- w_query: bfloat16 [2048, 2048], P(None, 'head'), may hold values from -0.61871843 to 0.61871843
- w_key: bfloat16 [2048, 2048], P(None, 'head'), may hold values from -0.61871843 to 0.61871843
- w_value: bfloat16 [2048, 2048], P(None, 'head'), may hold values from -0.61871843 to 0.61871843
- w_out: bfloat16 [2048, 2048], P('head'), may hold values from -0.61871843 to 0.61871843
- seeds: int32 [4], replicated, may hold values from 0 to 32748
Outputs:
- attended: bfloat16 [4096, 2048], P('seq', 'head')
- grad_tokens: bfloat16 [4096, 2048], P('seq', 'head')
- grad_w_query: float32 [2048, 2048], P('seq', 'head')
- grad_w_key: float32 [2048, 2048], P('seq', 'head')
- grad_w_value: float32 [2048, 2048], P('seq', 'head')
- grad_w_out: float32 [2048, 2048], P('head', 'seq')
The draws below stay inside these ranges and needn't reach their ends.
All inputs are finite; a program needn't handle non-finite values.
Results may differ from the reference program's by a relative error of at most 0.013.
The reference program's roundings to bfloat16 on the way count: a program that leaves them out, or rounds other values in their place, can miss the bound.
Values may be sent and summed in bfloat16 or wider, within the bound.
A program may use at most 192 MiB of HBM per device.

```python
import math
import jax
import jax.numpy as jnp
from jax import lax

D = 2048
HEADS = 16
DH = 128
LEAF = 128
TOKENS = 4096


def scaled_grid(key, row_total, col_total, low, high):
    key_base = jax.random.fold_in(key, 0)
    key_rows = jax.random.fold_in(key, 2)
    key_cols = jax.random.fold_in(key, 3)
    base_draw = jax.random.truncated_normal(key_base, -4.0, 4.0, (row_total, col_total), jnp.float32)
    blended = base_draw
    row_scale = jnp.exp(jax.random.uniform(key_rows, (row_total, 1), jnp.float32, math.log(low), math.log(high)))
    col_scale = jnp.exp(jax.random.uniform(key_cols, (1, col_total), jnp.float32, math.log(low), math.log(high)))
    return (blended * row_scale * col_scale / math.sqrt(row_total)).astype(jnp.bfloat16)


def draw_w_query(key, part):
    key = jax.random.fold_in(key, 11)
    return scaled_grid(key, D, D, 0.4, 2.5)


def draw_w_key(key, part):
    key = jax.random.fold_in(key, 23)
    return scaled_grid(key, D, D, 0.4, 2.5)


def draw_w_value(key, part):
    key = jax.random.fold_in(key, 37)
    return scaled_grid(key, D, D, 0.4, 2.5)


def draw_w_out(key, part):
    key = jax.random.fold_in(key, 41)
    return scaled_grid(key, D, D, 0.4, 2.5)


def place_ends(values, key, least, high):
    shape = values.shape
    place = [jax.random.randint(jax.random.fold_in(key, axis), (), 0, shape[axis]) for axis in range(len(shape))]
    values = values.at[tuple(place)].set(least)
    longest = shape.index(max(shape))
    place[longest] = (place[longest] + 1) % shape[longest]
    return values.at[tuple(place)].set(high)


def block_scale(rng, shape, cuts, least, high):
    factor_of, own = 1.0, jax.random.fold_in(rng, 6)
    for position, shards_of in cuts:
        draws = jnp.exp(jax.random.uniform(jax.random.fold_in(own, position), (shards_of,), jnp.float32, least / len(cuts), high / len(cuts)))
        factor_of = factor_of * jnp.repeat(draws, shape[position] // shards_of).reshape([-1 if axis == position else 1 for axis in range(len(shape))])
    return factor_of


def centred(key, shape, scale, reach, shards=(), kind=jnp.bfloat16):
    gain = block_scale(key, shape, shards, -0.22, 0.18) if shards else 1.0
    result = jax.random.normal(key, shape, jnp.float32) * scale * gain
    return jnp.minimum(jnp.maximum(result, -reach), reach).astype(kind)


def setup_inputs(seed: int = 0) -> dict:
    arg_keys = jax.random.split(jax.random.key(seed), 8)
    return {
        "tokens": centred(arg_keys[0], (TOKENS, D), 1.0, 6.0, ((0, 8),)),
        "cotangent": centred(arg_keys[1], (TOKENS, D), 1.0, 6.0, ((0, 8),)),
        "w_query": draw_w_query(jax.random.fold_in(arg_keys[7], 71), 0),
        "w_key": draw_w_key(jax.random.fold_in(arg_keys[7], 71), 0),
        "w_value": draw_w_value(jax.random.fold_in(arg_keys[7], 71), 0),
        "w_out": draw_w_out(jax.random.fold_in(arg_keys[7], 71), 0),
        "seeds": place_ends(jax.random.randint(arg_keys[6], (4,), 0, 32749), jax.random.fold_in(arg_keys[6], 1), 0, 32748).astype(jnp.int32),
    }


soft_cap = 6.0
noise_level = 0.5
prime_mod = 32749

def noise_grid(row_ids, col_ids, seed_value):
    row_part = row_ids[:, None]
    col_part = col_ids[None, :]
    hashed = (row_part * 7919 % prime_mod + col_part * 10007 % prime_mod + seed_value * 31337 % prime_mod) % prime_mod
    hashed = (hashed * hashed + col_part) % prime_mod
    hashed = (hashed * hashed + row_part) % prime_mod
    return hashed.astype(jnp.float32) * (2.0 / (prime_mod - 1)) - 1.0

def perturb(weight, noise, axis_no):
    as_float = weight.astype(jnp.float32)
    spread = jnp.sqrt(lax.optimization_barrier(jnp.mean(as_float * as_float, axis=axis_no, keepdims=True)) + 1e-06)
    return (as_float + noise_level * spread * noise).astype(jnp.bfloat16)

def halve_rows(rows_in):
    paired = rows_in.astype(jnp.float32).reshape((rows_in.shape[0] // 2, 2) + rows_in.shape[1:])
    return ((paired[:, 0] + paired[:, 1]) * 0.5).astype(jnp.bfloat16)

def expand_rows(grad_rows):
    return jnp.repeat(grad_rows * 0.5, 2, axis=0)

def flip_pairs(blocks):
    return blocks.reshape((blocks.shape[0] // 2, 2) + blocks.shape[1:])[:, ::-1].reshape(blocks.shape)

def group_view(array_in, groups):
    return array_in.reshape((groups, array_in.shape[0] // groups) + array_in.shape[1:])

def rounded(array_in):
    return lax.optimization_barrier(array_in.astype(jnp.bfloat16)).astype(jnp.float32)

def forward_set(queries, key_rows, value_rows, multiplicity):
    scale_q = 1.0 / math.sqrt(queries.shape[-1])
    scores = jnp.einsum('gqhd,gkhd->gqhk', queries.astype(jnp.float32), key_rows.astype(jnp.float32)) * scale_q
    capped = jnp.tanh(scores / soft_cap)
    weights = multiplicity * jnp.exp(soft_cap * capped)
    numerator = jnp.einsum('gqhk,gkhd->gqhd', rounded(weights), value_rows.astype(jnp.float32))
    return (lax.optimization_barrier(jnp.sum(weights, axis=-1)), numerator)

def backward_set(queries, key_rows, value_rows, grad_out, weight_sum, row_delta, multiplicity):
    scale_q = 1.0 / math.sqrt(queries.shape[-1])
    scores = jnp.einsum('gqhd,gkhd->gqhk', queries.astype(jnp.float32), key_rows.astype(jnp.float32)) * scale_q
    capped = jnp.tanh(scores / soft_cap)
    weights = multiplicity * jnp.exp(soft_cap * capped)
    probability = weights / weight_sum[..., None]
    grad_values = jnp.einsum('gqhk,gqhd->gkhd', rounded(probability), grad_out.astype(jnp.float32))
    grad_prob = jnp.einsum('gqhd,gkhd->gqhk', grad_out.astype(jnp.float32), value_rows.astype(jnp.float32))
    grad_scores = rounded(probability * (grad_prob - row_delta[..., None]) * (1.0 - capped * capped))
    grad_queries = jnp.einsum('gqhk,gkhd->gqhd', grad_scores, key_rows.astype(jnp.float32)) * scale_q
    grad_keys = jnp.einsum('gqhk,gqhd->gkhd', grad_scores, queries.astype(jnp.float32)) * scale_q
    return (grad_queries, grad_keys, grad_values)

def arrange(queries, key_rows, value_rows, flipped):
    groups = key_rows.shape[0] // LEAF
    key_view = group_view(key_rows, groups)
    value_view = group_view(value_rows, groups)
    if flipped:
        key_view = flip_pairs(key_view)
        value_view = flip_pairs(value_view)
    return (group_view(queries, groups), key_view, value_view, groups)

def reference(tokens, cotangent, w_query, w_key, w_value, w_out, seeds):
    all_ids = jnp.arange(D, dtype=jnp.int32)
    query_w = perturb(w_query, noise_grid(all_ids, all_ids, seeds[0]), 0)
    key_w = perturb(w_key, noise_grid(all_ids, all_ids, seeds[1]), 0)
    value_w = perturb(w_value, noise_grid(all_ids, all_ids, seeds[2]), 0)
    out_w = perturb(w_out, noise_grid(all_ids, all_ids, seeds[3]), 1)
    head_shape = (TOKENS, HEADS, DH)
    queries = jnp.dot(tokens, query_w, preferred_element_type=jnp.float32).astype(jnp.bfloat16).reshape(head_shape)
    key_all = jnp.dot(tokens, key_w, preferred_element_type=jnp.float32).astype(jnp.bfloat16).reshape(head_shape)
    value_all = jnp.dot(tokens, value_w, preferred_element_type=jnp.float32).astype(jnp.bfloat16).reshape(head_shape)
    levels = (TOKENS // LEAF).bit_length() - 1
    key_levels = [key_all]
    value_levels = [value_all]
    for level_no in range(1, levels):
        key_levels.append(halve_rows(key_levels[-1]))
        value_levels.append(halve_rows(value_levels[-1]))
    all_sets = [(0, False, 1.0)] + [(level_no, True, 2.0 ** level_no) for level_no in range(levels)]
    weight_sum = jnp.zeros((TOKENS, HEADS), jnp.float32)
    numerator = jnp.zeros(head_shape, jnp.float32)
    for level_no, flipped, multiplicity in all_sets:
        query_view, key_view, value_view, groups = arrange(queries, key_levels[level_no], value_levels[level_no], flipped)
        part_sum, part_num = forward_set(query_view, key_view, value_view, multiplicity)
        weight_sum = weight_sum + part_sum.reshape(TOKENS, HEADS)
        numerator = numerator + part_num.reshape(head_shape)
    attention = (numerator / weight_sum[..., None]).astype(jnp.bfloat16)
    flat_attention = attention.reshape(TOKENS, D)
    attended = jnp.dot(flat_attention, out_w, preferred_element_type=jnp.float32).astype(jnp.bfloat16)
    grad_attention = jnp.dot(cotangent, out_w.T, preferred_element_type=jnp.float32).astype(jnp.bfloat16)
    grad_heads = grad_attention.reshape(head_shape)
    row_delta = lax.optimization_barrier(jnp.sum(grad_heads.astype(jnp.float32) * attention.astype(jnp.float32), axis=-1))
    grad_q = jnp.zeros(head_shape, jnp.float32)
    key_grads = [jnp.zeros(k_rows.shape, jnp.float32) for k_rows in key_levels]
    value_grads = [jnp.zeros(v_rows.shape, jnp.float32) for v_rows in value_levels]
    for level_no, flipped, multiplicity in all_sets:
        query_view, key_view, value_view, groups = arrange(queries, key_levels[level_no], value_levels[level_no], flipped)
        dq_part, dk_part, dv_part = backward_set(query_view, key_view, value_view, group_view(grad_heads, groups), group_view(weight_sum, groups), group_view(row_delta, groups), multiplicity)
        grad_q = grad_q + dq_part.reshape(head_shape)
        if flipped:
            dk_part = flip_pairs(dk_part)
            dv_part = flip_pairs(dv_part)
        key_grads[level_no] = key_grads[level_no] + dk_part.reshape(key_levels[level_no].shape)
        value_grads[level_no] = value_grads[level_no] + dv_part.reshape(value_levels[level_no].shape)
    upper_k = key_grads[-1]
    upper_v = value_grads[-1]
    for level_no in reversed(range(levels - 1)):
        upper_k = key_grads[level_no] + expand_rows(upper_k)
        upper_v = value_grads[level_no] + expand_rows(upper_v)
    dq_flat = grad_q.astype(jnp.bfloat16).reshape(TOKENS, D)
    dk_flat = upper_k.astype(jnp.bfloat16).reshape(TOKENS, D)
    dv_flat = upper_v.astype(jnp.bfloat16).reshape(TOKENS, D)
    grads_cat = jnp.concatenate([dq_flat, dk_flat, dv_flat], axis=1)
    weights_cat = jnp.concatenate([query_w, key_w, value_w], axis=1)
    grad_tokens = jnp.dot(grads_cat, weights_cat.T, preferred_element_type=jnp.float32).astype(jnp.bfloat16)
    grad_w_query = jnp.dot(tokens.T, dq_flat, preferred_element_type=jnp.float32)
    grad_w_key = jnp.dot(tokens.T, dk_flat, preferred_element_type=jnp.float32)
    grad_w_value = jnp.dot(tokens.T, dv_flat, preferred_element_type=jnp.float32)
    grad_w_out = jnp.dot(flat_attention.T, cotangent, preferred_element_type=jnp.float32)
    return (attended, grad_tokens, grad_w_query, grad_w_key, grad_w_value, grad_w_out)
```

```python
import functools
import math

import jax
import jax.numpy as jnp
import numpy as np
from jax import lax
from jax.experimental import pallas as pl
from jax.experimental.pallas import tpu as pltpu
from jax.sharding import PartitionSpec as P

DH = 128
LEAF = 128
LANES = 128

soft_cap = 6.0
noise_level = 0.5
prime_mod = 32749
inv_prime = 1.0 / prime_mod
BF = jnp.bfloat16
F32 = jnp.float32


def centre(residue):
    return jnp.where(residue > prime_mod // 2, residue - prime_mod, residue)


def dot32(left, right):
    return jnp.dot(left, right, preferred_element_type=F32)


def dot_rows(left, right):
    return lax.dot_general(left, right, (((0,), (0,)), ((), ())), preferred_element_type=F32)


def perturb_kernel(axis_no, row_hash, row_id, col_hash, col_id, w_ref, out_ref):
    rows, cols = w_ref.shape
    chunk = min(rows, 256)
    if axis_no == 0:

        def add_squares(i, total):
            part = w_ref[pl.ds(pl.multiple_of(i * chunk, chunk), chunk), :].astype(F32)
            return total + jnp.sum(part * part, axis=0, keepdims=True)

        squares = lax.fori_loop(0, rows // chunk, add_squares, jnp.zeros((1, cols), F32))
        spread = noise_level * jnp.sqrt(squares * (1.0 / rows) + 1e-06)
    else:
        whole = w_ref[...].astype(F32)
        spread = noise_level * jnp.sqrt(
            jnp.sum(whole * whole, axis=1, keepdims=True) * (1.0 / cols) + 1e-06
        )
    step_u = spread * (2.0 / (prime_mod - 1))

    def do_rows(i, carry):
        here = pl.ds(pl.multiple_of(i * chunk, chunk), chunk)
        r_hash = row_hash[here, :]
        r_id = row_id[here, :]
        for j in range(cols // LANES):
            at = slice(j * LANES, (j + 1) * LANES)
            h = r_hash + col_hash[:, at]
            x = h * h + col_id[:, at]
            h = x - (x.astype(F32) * inv_prime).astype(jnp.int32) * prime_mod
            x = h * h + r_id
            h = x - (x.astype(F32) * inv_prime - 0.0078125).astype(jnp.int32) * prime_mod
            h = jnp.where(h >= prime_mod, h - prime_mod, h)
            if axis_no == 0:
                slope, base = step_u[:, at], spread[:, at]
            else:
                slope, base = step_u, spread
            out_ref[here, at] = (
                w_ref[here, at].astype(F32) + (h.astype(F32) * slope - base)
            ).astype(BF)
        return carry

    lax.fori_loop(0, rows // chunk, do_rows, 0)


def perturb(weight, row_hash, row_id, col_hash, col_id, axis_no):
    rows, cols = weight.shape
    if axis_no == 0:
        block = (rows, min(cols, 128))
        row_map, col_map, w_map = (lambda i: (0, 0)), (lambda i: (0, i)), (lambda i: (0, i))
        steps = cols // block[1]
    else:
        block = (min(rows, 128), cols)
        row_map, col_map, w_map = (lambda i: (i, 0)), (lambda i: (0, 0)), (lambda i: (i, 0))
        steps = rows // block[0]
    row_spec = pl.BlockSpec((block[0], LANES), row_map)
    col_spec = pl.BlockSpec((1, block[1]), col_map)
    return pl.pallas_call(
        functools.partial(perturb_kernel, axis_no),
        grid=(steps,),
        in_specs=[row_spec, row_spec, col_spec, col_spec, pl.BlockSpec(block, w_map)],
        out_specs=pl.BlockSpec(block, w_map),
        out_shape=jax.ShapeDtypeStruct((rows, cols), BF),
        compiler_params=pltpu.CompilerParams(vmem_limit_bytes=40 << 20),
        cost_estimate=pl.CostEstimate(
            flops=30 * rows * cols, bytes_accessed=4 * rows * cols, transcendentals=0
        ),
        name="perturb",
    )(row_hash, row_id, col_hash, col_id, weight)


def pair_mean(count):
    r = lax.broadcasted_iota(jnp.int32, (count // 2, count), 0)
    c = lax.broadcasted_iota(jnp.int32, (count // 2, count), 1)
    return jnp.where(c // 2 == r, 0.5, 0.0).astype(BF)


def coarse_kernel(k_ref, v_ref, *outs):
    cols = k_ref.shape[1]
    for n, src in enumerate((k_ref, v_ref)):
        rows = src[...]
        for out in outs:
            count = rows.shape[0]
            if count >= 16:
                rows = dot32(pair_mean(count), rows).astype(BF)
            out[:, n * cols : (n + 1) * cols] = rows


def attention_kernel(
    tok_rows,
    cross_rows,
    q_ref,
    k_ref,
    v_ref,
    do_ref,
    k1_ref,
    v1_ref,
    kx_ref,
    vx_ref,
    att_ref,
    dq_ref,
    dk_ref,
    dv_ref,
    dkx_ref,
    dvx_ref,
):
    pair = 2 * LEAF
    groups = tok_rows // pair
    scale_q = 1.0 / math.sqrt(DH)
    total_keys = pair + LEAF + cross_rows
    rows = lax.broadcasted_iota(jnp.int32, (total_keys, 1), 0)
    log_m = jnp.where(rows < pair, 0, (rows - pair) // LEAF + 1).astype(F32)
    dk1 = [None] * groups
    dv1 = [None] * groups
    dkx = None
    dvx = None
    for g in range(groups):
        own = slice(g * pair, (g + 1) * pair)
        other = slice((g ^ 1) * LEAF, ((g ^ 1) + 1) * LEAF)
        keys = jnp.concatenate([k_ref[own, :], k1_ref[other, :], kx_ref[...]], axis=0)
        values = jnp.concatenate([v_ref[own, :], v1_ref[other, :], vx_ref[...]], axis=0)
        q = q_ref[own, :]
        do = do_ref[own, :]
        do_t = do.astype(F32).T
        s = dot32(keys, q.astype(F32).T.astype(BF))
        t = jnp.tanh(s * (scale_q / soft_cap))
        w = jnp.exp2(t * (soft_cap * math.log2(math.e)) + log_m)
        weight_sum = jnp.sum(w, axis=0, keepdims=True)
        values_t = values.astype(F32).T.astype(BF)
        att_t = (dot32(values_t, w.astype(BF)) / weight_sum).astype(BF).astype(F32)
        att_ref[own, :] = att_t.T.astype(BF)
        delta = jnp.sum(att_t * do_t, axis=0, keepdims=True)
        p = w * (1.0 / weight_sum)
        dv = dot32(p.astype(BF), do)
        dp = dot32(values, do_t.astype(BF))
        grad = (p * (dp - delta) * (1.0 - t * t)).astype(BF)
        dk = dot32(grad, q) * scale_q
        keys_t = keys.astype(F32).T.astype(BF)
        dq_ref[own, :] = (dot32(keys_t, grad) * scale_q).T.astype(BF)
        dk_ref[own, :] = dk[:pair]
        dv_ref[own, :] = dv[:pair]
        dk1[g ^ 1] = dk[pair : pair + LEAF]
        dv1[g ^ 1] = dv[pair : pair + LEAF]
        dkx = dk[pair + LEAF :] if dkx is None else dkx + dk[pair + LEAF :]
        dvx = dv[pair + LEAF :] if dvx is None else dvx + dv[pair + LEAF :]
    r = lax.broadcasted_iota(jnp.int32, (pair, LEAF), 0)
    c = lax.broadcasted_iota(jnp.int32, (pair, LEAF), 1)
    expand = jnp.where(r // 2 == c, 0.5, 0.0).astype(BF)
    for g in range(groups):
        own = slice(g * pair, (g + 1) * pair)
        for ref, upper in ((dk_ref, dk1[g]), (dv_ref, dv1[g])):
            high = upper.astype(BF)
            low = (upper - high.astype(F32)).astype(BF)
            ref[own, :] += dot32(expand, high) + dot32(expand, low)
    dkx_ref[...] = dkx.astype(BF)
    dvx_ref[...] = dvx.astype(BF)


def fused_attention(q, k, v, do, kv1, kvx):
    tok_rows, cols = q.shape
    heads = cols // DH
    cross_rows = kvx.shape[0]

    def spec(rows, shift=0):
        return pl.BlockSpec((rows, DH), lambda h: (0, h + shift))

    out_shape = [
        jax.ShapeDtypeStruct((tok_rows, cols), BF),
        jax.ShapeDtypeStruct((tok_rows, cols), BF),
        jax.ShapeDtypeStruct((tok_rows, cols), F32),
        jax.ShapeDtypeStruct((tok_rows, cols), F32),
        jax.ShapeDtypeStruct((cross_rows, cols), BF),
        jax.ShapeDtypeStruct((cross_rows, cols), BF),
    ]
    scores = tok_rows * (3 * LEAF + cross_rows) * heads
    return pl.pallas_call(
        functools.partial(attention_kernel, tok_rows, cross_rows),
        grid=(heads,),
        in_specs=[spec(tok_rows)] * 4
        + [spec(kv1.shape[0]), spec(kv1.shape[0], heads)]
        + [spec(cross_rows), spec(cross_rows, heads)],
        out_specs=[spec(tok_rows)] * 4 + [spec(cross_rows)] * 2,
        out_shape=out_shape,
        compiler_params=pltpu.CompilerParams(vmem_limit_bytes=48 << 20),
        cost_estimate=pl.CostEstimate(
            flops=12 * scores * DH, bytes_accessed=16 * tok_rows * cols, transcendentals=2 * scores
        ),
        name="attention",
    )(q, k, v, do, kv1, kv1, kvx, kvx)


def cross_rows_of(apart):
    return LEAF >> (apart.bit_length() - 1)


def upper_matrix(tok_rows, seq_count):
    parts = []
    for apart in range(1, seq_count):
        count = cross_rows_of(apart)
        wide = tok_rows // count
        parts.append(np.kron(np.eye(count), np.ones((wide, 1))) / wide)
    return jnp.asarray(np.concatenate(parts, axis=1), BF)


def body(tokens, cotangent, w_query, w_key, w_value, w_out, seeds):
    seq_count = lax.axis_size("seq")
    head_count = lax.axis_size("head")
    seq_bits = seq_count.bit_length() - 1
    seq_idx = lax.axis_index("seq")
    head_idx = lax.axis_index("head")
    tok_rows, model_width = tokens.shape
    head_cols = w_query.shape[1]
    outer = seq_count // 2
    share = model_width // seq_count
    inner_idx = seq_idx % 2
    outer_idx = seq_idx // 2

    def swapped(array, axis, apart):
        return lax.ppermute(
            array, axis, [(i, i ^ apart) for i in range(lax.axis_size(axis))]
        )

    def half_of(array, which):
        view = array.reshape(tok_rows, outer, 2, share)
        return jnp.where(which == 0, view[:, :, 0], view[:, :, 1]).reshape(tok_rows, outer * share)

    tok_mine, cot_mine = half_of(tokens, inner_idx), half_of(cotangent, inner_idx)
    tok_pair = swapped(half_of(tokens, 1 - inner_idx), "seq", 1)
    cot_pair = swapped(half_of(cotangent, 1 - inner_idx), "seq", 1)

    all_ids = jnp.arange(model_width, dtype=jnp.int32)
    own_ids = head_idx * head_cols + jnp.arange(head_cols, dtype=jnp.int32)

    def over_lanes(vector):
        return jnp.broadcast_to(vector[:, None], (vector.shape[0], LANES))

    def hash_rows(ids):
        return over_lanes(centre(ids * 7919 % prime_mod))

    def hash_cols(ids, seed):
        seeded = (ids * 10007 % prime_mod + seed * 31337 % prime_mod) % prime_mod
        return centre(seeded)[None, :]

    all_hash, all_rows = hash_rows(all_ids), over_lanes(all_ids)
    own_hash, own_rows = hash_rows(own_ids), over_lanes(own_ids)

    def perturb_in(weight, n):
        return perturb(
            weight, all_hash, all_rows, hash_cols(own_ids, seeds[n]), own_ids[None, :], 0
        )

    key_w = perturb_in(w_key, 1)
    value_w = perturb_in(w_value, 2)
    keys = dot32(tokens, key_w).astype(BF)
    values = dot32(tokens, value_w).astype(BF)

    levels = 1 + seq_bits
    coarse = pl.pallas_call(
        coarse_kernel,
        out_shape=[
            jax.ShapeDtypeStruct((tok_rows >> n + 1, 2 * head_cols), BF) for n in range(levels)
        ],
        name="coarse",
    )(keys, values)
    kvx = jnp.concatenate(
        [swapped(coarse[d.bit_length()], "seq", d) for d in range(1, seq_count)], axis=0
    )

    query_w = perturb_in(w_query, 0)
    queries = dot32(tokens, query_w).astype(BF)
    out_w = perturb(w_out, own_hash, own_rows, hash_cols(all_ids, seeds[3]), all_ids[None, :], 1)
    grad_att = lax.dot_general(
        cotangent, out_w, (((1,), (1,)), ((), ())), preferred_element_type=F32
    ).astype(BF)

    att, dq, dk_own, dv_own, dkx, dvx = fused_attention(
        queries, keys, values, grad_att, coarse[0], kvx
    )

    returned = []
    at = 0
    dkvx = jnp.concatenate([dkx, dvx], axis=1)
    for apart in range(1, seq_count):
        count = cross_rows_of(apart)
        returned.append(swapped(dkvx[at : at + count], "seq", apart))
        at += count

    dq_pair = swapped(dq, "seq", 1)
    att_pair = swapped(att, "seq", 1)

    def sum_heads(terms):
        def piece(apart):
            return lax.dynamic_slice_in_dim(
                terms, (head_idx ^ apart) * head_cols, head_cols, axis=1
            )

        total = piece(0)
        for apart in range(1, head_count):
            total = total + swapped(piece(apart).astype(BF), "head", apart).astype(F32)
        return total.astype(BF)

    def reduce_chain(left, left_pair, right, right_pair, flip):
        def chunk(n):
            n = jnp.clip(n, 0, outer - 1) * share
            a = lax.dynamic_slice_in_dim(left, n, share, axis=1)
            b = lax.dynamic_slice_in_dim(left_pair, n, share, axis=1)
            if flip:
                return dot_rows(right, a) + dot_rows(right_pair, b)
            return dot_rows(a, right) + dot_rows(b, right_pair)

        up = down = None
        for t in range(1, outer):
            up_part = chunk(outer_idx + outer - t)
            down_part = chunk(outer_idx + t - outer)
            if up is not None:
                up_part = up_part + up.astype(F32)
                down_part = down_part + down.astype(F32)
            up_pairs = [(2 * z + x, 2 * z + 2 + x) for z in range(t) for x in range(2)]
            down_pairs = [
                (2 * z + x, 2 * z - 2 + x) for z in range(outer - t, outer) for x in range(2)
            ]
            up = lax.ppermute(up_part.astype(BF), "seq", up_pairs)
            down = lax.ppermute(down_part.astype(BF), "seq", down_pairs)
        own = chunk(outer_idx)
        if up is not None:
            own = own + up.astype(F32) + down.astype(F32)
        return own

    grad_w_out = reduce_chain(cot_mine, cot_pair, att, att_pair, True)
    grad_w_query = reduce_chain(tok_mine, tok_pair, dq, dq_pair, False)
    attended = sum_heads(dot32(att, out_w))

    upper = dot32(upper_matrix(tok_rows, seq_count), jnp.concatenate(returned, axis=0))
    dk = (dk_own + upper[:, :head_cols]).astype(BF)
    dv = (dv_own + upper[:, head_cols:]).astype(BF)
    dk_pair = swapped(dk, "seq", 1)
    dv_pair = swapped(dv, "seq", 1)

    def back(grad, weight):
        return lax.dot_general(grad, weight, (((1,), (1,)), ((), ())), preferred_element_type=F32)

    grad_tokens = sum_heads(back(dq, query_w) + back(dk, key_w) + back(dv, value_w))
    grad_w_key = reduce_chain(tok_mine, tok_pair, dk, dk_pair, False)
    grad_w_value = reduce_chain(tok_mine, tok_pair, dv, dv_pair, False)
    return (attended, grad_tokens, grad_w_query, grad_w_key, grad_w_value, grad_w_out)


def solution(mesh):
    in_specs = (
        P("seq", None),
        P("seq", None),
        P(None, "head"),
        P(None, "head"),
        P(None, "head"),
        P("head", None),
        P(),
    )
    out_specs = (
        P("seq", "head"),
        P("seq", "head"),
        P("seq", "head"),
        P("seq", "head"),
        P("seq", "head"),
        P("head", "seq"),
    )
    return jax.shard_map(body, mesh=mesh, in_specs=in_specs, out_specs=out_specs, check_vma=False)
```

```python
import functools
import math

import jax
import jax.numpy as jnp
import numpy as np
from jax import lax
from jax.experimental import pallas as pl
from jax.experimental.pallas import tpu as pltpu
from jax.sharding import PartitionSpec as P

DH = 128
LEAF = 128
LANES = 128

soft_cap = 6.0
noise_level = 0.5
prime_mod = 32749
inv_prime = 1.0 / prime_mod
BF = jnp.bfloat16
F32 = jnp.float32


def centre(residue):
    return jnp.where(residue > prime_mod // 2, residue - prime_mod, residue)


def dot32(left, right):
    return jnp.dot(left, right, preferred_element_type=F32)


def perturb_kernel(axis_no, row_hash, row_id, col_hash, col_id, w_ref, out_ref):
    rows, cols = w_ref.shape
    chunk = min(rows, 256)
    if axis_no == 0:

        def add_squares(i, total):
            part = w_ref[pl.ds(pl.multiple_of(i * chunk, chunk), chunk), :].astype(F32)
            return total + jnp.sum(part * part, axis=0, keepdims=True)

        squares = lax.fori_loop(0, rows // chunk, add_squares, jnp.zeros((1, cols), F32))
        spread = noise_level * jnp.sqrt(squares * (1.0 / rows) + 1e-06)
    else:
        whole = w_ref[...].astype(F32)
        spread = noise_level * jnp.sqrt(
            jnp.sum(whole * whole, axis=1, keepdims=True) * (1.0 / cols) + 1e-06
        )
    step_u = spread * (2.0 / (prime_mod - 1))

    def do_rows(i, carry):
        here = pl.ds(pl.multiple_of(i * chunk, chunk), chunk)
        r_hash = row_hash[here, :]
        r_id = row_id[here, :]
        for j in range(cols // LANES):
            at = slice(j * LANES, (j + 1) * LANES)
            h = r_hash + col_hash[:, at]
            x = h * h + col_id[:, at]
            h = x - (x.astype(F32) * inv_prime).astype(jnp.int32) * prime_mod
            x = h * h + r_id
            h = x - (x.astype(F32) * inv_prime - 0.0078125).astype(jnp.int32) * prime_mod
            h = jnp.where(h >= prime_mod, h - prime_mod, h)
            if axis_no == 0:
                slope, base = step_u[:, at], spread[:, at]
            else:
                slope, base = step_u, spread
            out_ref[here, at] = (
                w_ref[here, at].astype(F32) + (h.astype(F32) * slope - base)
            ).astype(BF)
        return carry

    lax.fori_loop(0, rows // chunk, do_rows, 0)


def perturb(weight, row_hash, row_id, col_hash, col_id, axis_no):
    rows, cols = weight.shape
    if axis_no == 0:
        block = (rows, min(cols, 128))
        row_map, col_map, w_map = (lambda i: (0, 0)), (lambda i: (0, i)), (lambda i: (0, i))
        steps = cols // block[1]
    else:
        block = (min(rows, 128), cols)
        row_map, col_map, w_map = (lambda i: (i, 0)), (lambda i: (0, 0)), (lambda i: (i, 0))
        steps = rows // block[0]
    row_spec = pl.BlockSpec((block[0], LANES), row_map)
    col_spec = pl.BlockSpec((1, block[1]), col_map)
    return pl.pallas_call(
        functools.partial(perturb_kernel, axis_no),
        grid=(steps,),
        in_specs=[row_spec, row_spec, col_spec, col_spec, pl.BlockSpec(block, w_map)],
        out_specs=pl.BlockSpec(block, w_map),
        out_shape=jax.ShapeDtypeStruct((rows, cols), BF),
        compiler_params=pltpu.CompilerParams(vmem_limit_bytes=40 << 20),
        cost_estimate=pl.CostEstimate(
            flops=30 * rows * cols, bytes_accessed=4 * rows * cols, transcendentals=0
        ),
        name="perturb",
    )(row_hash, row_id, col_hash, col_id, weight)


def pair_mean(count):
    r = lax.broadcasted_iota(jnp.int32, (count // 2, count), 0)
    c = lax.broadcasted_iota(jnp.int32, (count // 2, count), 1)
    return jnp.where(c // 2 == r, 0.5, 0.0).astype(BF)


def coarse_kernel(k_ref, v_ref, *outs):
    cols = k_ref.shape[1]
    for n, src in enumerate((k_ref, v_ref)):
        rows = src[...]
        for out in outs:
            count = rows.shape[0]
            if count >= 16:
                rows = dot32(pair_mean(count), rows).astype(BF)
            out[:, n * cols : (n + 1) * cols] = rows


def attention_kernel(
    tok_rows,
    cross_rows,
    q_ref,
    k_ref,
    v_ref,
    do_ref,
    k1_ref,
    v1_ref,
    kx_ref,
    vx_ref,
    att_ref,
    dq_ref,
    dk_ref,
    dv_ref,
    dkvx_ref,
):
    pair = 2 * LEAF
    groups = tok_rows // pair
    scale_q = 1.0 / math.sqrt(DH)
    total_keys = pair + LEAF + cross_rows
    rows = lax.broadcasted_iota(jnp.int32, (total_keys, 1), 0)
    log_m = jnp.where(rows < pair, 0, (rows - pair) // LEAF + 1).astype(F32)
    dk1 = [None] * groups
    dv1 = [None] * groups
    dkx = None
    dvx = None
    for g in range(groups):
        own = slice(g * pair, (g + 1) * pair)
        other = slice((g ^ 1) * LEAF, ((g ^ 1) + 1) * LEAF)
        keys = jnp.concatenate([k_ref[own, :], k1_ref[other, :], kx_ref[...]], axis=0)
        values = jnp.concatenate([v_ref[own, :], v1_ref[other, :], vx_ref[...]], axis=0)
        q = q_ref[own, :]
        do = do_ref[own, :]
        do_t = do.astype(F32).T
        s = dot32(keys, q.astype(F32).T.astype(BF))
        t = jnp.tanh(s * (scale_q / soft_cap))
        w = jnp.exp2(t * (soft_cap * math.log2(math.e)) + log_m)
        weight_sum = jnp.sum(w, axis=0, keepdims=True)
        values_t = values.astype(F32).T.astype(BF)
        att_t = (dot32(values_t, w.astype(BF)) / weight_sum).astype(BF).astype(F32)
        att_ref[own, :] = att_t.T.astype(BF)
        delta = jnp.sum(att_t * do_t, axis=0, keepdims=True)
        p = w * (1.0 / weight_sum)
        dv = dot32(p.astype(BF), do)
        dp = dot32(values, do_t.astype(BF))
        grad = (p * (dp - delta) * (1.0 - t * t)).astype(BF)
        dk = dot32(grad, q) * scale_q
        keys_t = keys.astype(F32).T.astype(BF)
        dq_ref[own, :] = (dot32(keys_t, grad) * scale_q).T.astype(BF)
        dk_ref[own, :] = dk[:pair]
        dv_ref[own, :] = dv[:pair]
        dk1[g ^ 1] = dk[pair : pair + LEAF]
        dv1[g ^ 1] = dv[pair : pair + LEAF]
        dkx = dk[pair + LEAF :] if dkx is None else dkx + dk[pair + LEAF :]
        dvx = dv[pair + LEAF :] if dvx is None else dvx + dv[pair + LEAF :]
    r = lax.broadcasted_iota(jnp.int32, (pair, LEAF), 0)
    c = lax.broadcasted_iota(jnp.int32, (pair, LEAF), 1)
    expand = jnp.where(r // 2 == c, 0.5, 0.0).astype(BF)
    for g in range(groups):
        own = slice(g * pair, (g + 1) * pair)
        for ref, upper in ((dk_ref, dk1[g]), (dv_ref, dv1[g])):
            high = upper.astype(BF)
            low = (upper - high.astype(F32)).astype(BF)
            ref[own, :] += dot32(expand, high) + dot32(expand, low)
    dkvx_ref[0] = dkx.astype(BF)
    dkvx_ref[1] = dvx.astype(BF)


def fused_attention(q, k, v, do, kv1, kvx):
    tok_rows, cols = q.shape
    heads = cols // DH
    cross_rows = kvx.shape[0]

    def spec(rows, shift=0):
        return pl.BlockSpec((rows, DH), lambda h: (0, h + shift))

    out_shape = [
        jax.ShapeDtypeStruct((tok_rows, cols), BF),
        jax.ShapeDtypeStruct((tok_rows, cols), BF),
        jax.ShapeDtypeStruct((tok_rows, cols), F32),
        jax.ShapeDtypeStruct((tok_rows, cols), F32),
        jax.ShapeDtypeStruct((2, cross_rows, cols), BF),
    ]
    scores = tok_rows * (3 * LEAF + cross_rows) * heads
    return pl.pallas_call(
        functools.partial(attention_kernel, tok_rows, cross_rows),
        grid=(heads,),
        in_specs=[spec(tok_rows)] * 4
        + [spec(kv1.shape[0]), spec(kv1.shape[0], heads)]
        + [spec(cross_rows), spec(cross_rows, heads)],
        out_specs=[spec(tok_rows)] * 4
        + [pl.BlockSpec((2, cross_rows, DH), lambda h: (0, 0, h))],
        out_shape=out_shape,
        compiler_params=pltpu.CompilerParams(vmem_limit_bytes=48 << 20),
        cost_estimate=pl.CostEstimate(
            flops=12 * scores * DH, bytes_accessed=16 * tok_rows * cols, transcendentals=2 * scores
        ),
        name="attention",
    )(q, k, v, do, kv1, kv1, kvx, kvx)


def cross_rows_of(apart):
    return LEAF >> (apart.bit_length() - 1)


def upper_matrix(tok_rows, seq_count):
    parts = []
    for apart in range(1, seq_count):
        count = cross_rows_of(apart)
        wide = tok_rows // count
        parts.append(np.kron(np.eye(count), np.ones((wide, 1))) / wide)
    return jnp.asarray(np.concatenate(parts, axis=1), BF)


def flipped(idx, apart):
    peer = idx
    for bit in range(apart.bit_length()):
        if apart >> bit & 1:
            peer = peer + (1 << bit) * (1 - 2 * (idx // (1 << bit) % 2))
    return peer


def dot_nt(left, right):
    return lax.dot_general(left, right, (((1,), (1,)), ((), ())), preferred_element_type=F32)


def tail_kernel(
    seq_count,
    head_count,
    att_ref,
    dq_ref,
    dk_own_ref,
    dv_own_ref,
    dkvx_ref,
    upper_ref,
    tok_ref,
    tok_pair_ref,
    cot_ref,
    cot_pair_ref,
    wq_ref,
    wk_ref,
    wv_ref,
    wo_ref,
    attended_ref,
    grad_tok_ref,
    gq_ref,
    gk_ref,
    gv_ref,
    go_ref,
    grads,
    pairs,
    back_in,
    head_out,
    head_in,
    chain_out,
    up_in,
    down_in,
    pair_send,
    pair_recv,
    back_send,
    back_recv,
    head_send,
    head_recv,
    chain_send,
    up_recv,
    down_recv,
):
    seq_idx = lax.axis_index("seq")
    head_idx = lax.axis_index("head")
    outer = seq_count // 2
    z = seq_idx // 2
    partner = flipped(seq_idx, 1)
    head_cols = att_ref.shape[1]

    barrier = pltpu.get_barrier_semaphore()
    for apart in range(1, seq_count):
        pl.semaphore_signal(
            barrier,
            inc=1,
            device_id={"seq": flipped(seq_idx, apart)},
            device_id_type=pl.DeviceIdType.MESH,
        )
    for apart in range(1, head_count):
        pl.semaphore_signal(
            barrier,
            inc=1,
            device_id={"head": (head_idx + apart) % head_count},
            device_id_type=pl.DeviceIdType.MESH,
        )
    pl.semaphore_wait(barrier, seq_count + head_count - 2)

    def remote(src, dst, send_sem, recv_sem, axis, peer):
        return pltpu.make_async_remote_copy(
            src_ref=src,
            dst_ref=dst,
            send_sem=send_sem,
            recv_sem=recv_sem,
            device_id={axis: peer},
            device_id_type=pl.DeviceIdType.MESH,
        )

    backs = []
    at = 0
    for apart in range(1, seq_count):
        rows = pl.ds(at, cross_rows_of(apart))
        at += cross_rows_of(apart)
        backs.append(
            remote(
                dkvx_ref.at[:, rows, :],
                back_in.at[:, rows, :],
                back_send.at[apart],
                back_recv.at[apart],
                "seq",
                flipped(seq_idx, apart),
            )
        )
    for copy in backs:
        copy.start()

    sources = (dq_ref, att_ref, grads.at[0], grads.at[1])
    lefts = (tok_ref, cot_ref, tok_ref, tok_ref)
    left_pairs = (tok_pair_ref, cot_pair_ref, tok_pair_ref, tok_pair_ref)
    outs = (gq_ref, go_ref, gk_ref, gv_ref)
    pair_copies = [
        remote(sources[n], pairs.at[n], pair_send.at[n], pair_recv.at[n], "seq", partner)
        for n in range(4)
    ]
    pair_copies[0].start()
    pair_copies[1].start()

    def send_terms(which, term, result_ref):
        copies = []
        for apart in range(1, head_count):
            peer = (head_idx + apart) % head_count
            head_out[which, apart - 1] = term(peer).astype(BF)
            copy = remote(
                head_out.at[which, apart - 1],
                head_in.at[which, apart - 1],
                head_send.at[which, apart - 1],
                head_recv.at[which, apart - 1],
                "head",
                peer,
            )
            copy.start()
            copies.append(copy)
        return copies

    def finish_terms(which, term, copies, result_ref):
        total = term(head_idx)
        for apart, copy in enumerate(copies):
            copy.wait()
            total = total + head_in[which, apart].astype(F32)
        result_ref[...] = total.astype(BF)

    def piece(n):
        return pl.ds(pl.multiple_of(n * head_cols, head_cols), head_cols)

    def out_term(n):
        return dot32(att_ref[...], wo_ref[:, piece(n)])

    def in_term(n):
        return (
            dot_nt(dq_ref[...], wq_ref[piece(n), :])
            + dot_nt(grads[0], wk_ref[piece(n), :])
            + dot_nt(grads[1], wv_ref[piece(n), :])
        )

    def partial(n, c):
        return dot32(lefts[n][c], sources[n][...]) + dot32(left_pairs[n][c], pairs[n])

    def up_copy(n, c):
        return remote(
            chain_out.at[n, c], up_in.at[n, c], chain_send.at[n, c], up_recv.at[n, c],
            "seq", (seq_idx + 2) % seq_count,
        )

    def down_copy(n, c):
        return remote(
            chain_out.at[n, c], down_in.at[n, c], chain_send.at[n, c], down_recv.at[n, c],
            "seq", (seq_idx + seq_count - 2) % seq_count,
        )

    def chain(n):
        pair_copies[n].wait_recv()

        def step(t, carry):
            @pl.when(z <= t - 1)
            def _():
                c = z + outer - t
                chain_out[n, c] = partial(n, c).astype(BF)

                @pl.when(z > 0)
                def _():
                    up_copy(n, c).wait_recv()
                    chain_out[n, c] = (
                        chain_out[n, c].astype(F32) + up_in[n, c].astype(F32)
                    ).astype(BF)

                up_copy(n, c).start()

            @pl.when(z >= outer - t)
            def _():
                c = z + t - outer
                chain_out[n, c] = partial(n, c).astype(BF)

                @pl.when(z < outer - 1)
                def _():
                    down_copy(n, c).wait_recv()
                    chain_out[n, c] = (
                        chain_out[n, c].astype(F32) + down_in[n, c].astype(F32)
                    ).astype(BF)

                down_copy(n, c).start()

            return carry

        lax.fori_loop(1, outer, step, 0)

    def finish_chain(n):
        own = partial(n, z)

        def store(total):
            outs[n][...] = total.T if n == 1 else total

        @pl.when(z == 0)
        def _():
            down_copy(n, z).wait_recv()
            store(own + down_in[n, z].astype(F32))

        @pl.when(z == outer - 1)
        def _():
            up_copy(n, z).wait_recv()
            store(own + up_in[n, z].astype(F32))

        @pl.when((z > 0) & (z < outer - 1))
        def _():
            up_copy(n, z).wait_recv()
            down_copy(n, z).wait_recv()
            store(own + up_in[n, z].astype(F32) + down_in[n, z].astype(F32))

    att_copies = send_terms(0, out_term, attended_ref)
    for copy in backs:
        copy.wait_recv()
    grads[0] = (dk_own_ref[...] + dot32(upper_ref[...], back_in[0])).astype(BF)
    grads[1] = (dv_own_ref[...] + dot32(upper_ref[...], back_in[1])).astype(BF)
    pair_copies[2].start()
    pair_copies[3].start()
    chain(0)
    tok_copies = send_terms(1, in_term, grad_tok_ref)
    chain(1)
    finish_chain(0)
    chain(2)
    finish_terms(0, out_term, att_copies, attended_ref)
    finish_chain(1)
    chain(3)
    finish_terms(1, in_term, tok_copies, grad_tok_ref)
    finish_chain(2)
    finish_chain(3)
    for copy in backs + pair_copies:
        copy.wait_send()

    def drain(c, carry):
        @pl.when(c != z)
        def _():
            for n in range(4):
                up_copy(n, c).wait_send()

        return carry

    lax.fori_loop(0, outer, drain, 0)


def tail(seq_count, head_count, *arrays):
    att, dkvx, tok = arrays[0], arrays[4], arrays[6]
    tok_rows, head_cols = att.shape
    outer, share = tok.shape[:2]
    vmem = pl.BlockSpec(memory_space=pltpu.VMEM)
    chunk = (4, outer, share, head_cols)
    grad = jax.ShapeDtypeStruct((share, head_cols), F32)
    tokens_out = jax.ShapeDtypeStruct((tok_rows, head_cols), BF)
    dma = pltpu.SemaphoreType.DMA
    return pl.pallas_call(
        functools.partial(tail_kernel, seq_count, head_count),
        in_specs=[vmem] * len(arrays),
        out_specs=[vmem] * 6,
        out_shape=[tokens_out] * 2
        + [grad] * 3
        + [jax.ShapeDtypeStruct((head_cols, share), F32)],
        scratch_shapes=[
            pltpu.VMEM((2, tok_rows, head_cols), BF),
            pltpu.VMEM((4, tok_rows, head_cols), BF),
            pltpu.VMEM(dkvx.shape, BF),
            pltpu.VMEM((2, head_count - 1, tok_rows, head_cols), BF),
            pltpu.VMEM((2, head_count - 1, tok_rows, head_cols), BF),
            pltpu.VMEM(chunk, BF),
            pltpu.VMEM(chunk, BF),
            pltpu.VMEM(chunk, BF),
            dma((4,)),
            dma((4,)),
            dma((seq_count,)),
            dma((seq_count,)),
            dma((2, head_count - 1)),
            dma((2, head_count - 1)),
            dma((4, outer)),
            dma((4, outer)),
            dma((4, outer)),
        ],
        compiler_params=pltpu.CompilerParams(
            collective_id=0, has_side_effects=True, vmem_limit_bytes=58 << 20
        ),
        cost_estimate=pl.CostEstimate(
            flops=20 * tok_rows * head_cols * share * outer,
            bytes_accessed=32 << 20,
            transcendentals=0,
        ),
        name="tail",
    )(*arrays)


def body(tokens, cotangent, w_query, w_key, w_value, w_out, seeds):
    seq_count = lax.axis_size("seq")
    head_count = lax.axis_size("head")
    seq_bits = seq_count.bit_length() - 1
    seq_idx = lax.axis_index("seq")
    head_idx = lax.axis_index("head")
    tok_rows, model_width = tokens.shape
    head_cols = w_query.shape[1]
    outer = seq_count // 2
    share = model_width // seq_count
    inner_idx = seq_idx % 2

    def swapped(array, axis, apart):
        return lax.ppermute(
            array, axis, [(i, i ^ apart) for i in range(lax.axis_size(axis))]
        )

    def half_of(array, which):
        view = array.T.reshape(outer, 2, share, tok_rows)
        return jnp.where(which == 0, view[:, 0], view[:, 1])

    tok_mine, cot_mine = half_of(tokens, inner_idx), half_of(cotangent, inner_idx)
    tok_pair = swapped(half_of(tokens, 1 - inner_idx), "seq", 1)
    cot_pair = swapped(half_of(cotangent, 1 - inner_idx), "seq", 1)

    all_ids = jnp.arange(model_width, dtype=jnp.int32)
    own_ids = head_idx * head_cols + jnp.arange(head_cols, dtype=jnp.int32)

    def over_lanes(vector):
        return jnp.broadcast_to(vector[:, None], (vector.shape[0], LANES))

    def hash_rows(ids):
        return over_lanes(centre(ids * 7919 % prime_mod))

    def hash_cols(ids, seed):
        seeded = (ids * 10007 % prime_mod + seed * 31337 % prime_mod) % prime_mod
        return centre(seeded)[None, :]

    all_hash, all_rows = hash_rows(all_ids), over_lanes(all_ids)
    own_hash, own_rows = hash_rows(own_ids), over_lanes(own_ids)

    def perturb_in(weight, n):
        return perturb(
            weight, all_hash, all_rows, hash_cols(own_ids, seeds[n]), own_ids[None, :], 0
        )

    key_w = perturb_in(w_key, 1)
    value_w = perturb_in(w_value, 2)
    keys = dot32(tokens, key_w).astype(BF)
    values = dot32(tokens, value_w).astype(BF)

    levels = 1 + seq_bits
    coarse = pl.pallas_call(
        coarse_kernel,
        out_shape=[
            jax.ShapeDtypeStruct((tok_rows >> n + 1, 2 * head_cols), BF) for n in range(levels)
        ],
        name="coarse",
    )(keys, values)
    kvx = jnp.concatenate(
        [swapped(coarse[d.bit_length()], "seq", d) for d in range(1, seq_count)], axis=0
    )

    query_w = perturb_in(w_query, 0)
    queries = dot32(tokens, query_w).astype(BF)
    out_w = perturb(w_out, own_hash, own_rows, hash_cols(all_ids, seeds[3]), all_ids[None, :], 1)
    grad_att = lax.dot_general(
        cotangent, out_w, (((1,), (1,)), ((), ())), preferred_element_type=F32
    ).astype(BF)

    att, dq, dk_own, dv_own, dkvx = fused_attention(
        queries, keys, values, grad_att, coarse[0], kvx
    )
    attended, grad_tokens, grad_w_query, grad_w_key, grad_w_value, grad_w_out = tail(
        seq_count,
        head_count,
        att,
        dq,
        dk_own,
        dv_own,
        dkvx,
        upper_matrix(tok_rows, seq_count),
        tok_mine,
        tok_pair,
        cot_mine,
        cot_pair,
        query_w,
        key_w,
        value_w,
        out_w,
    )
    return (attended, grad_tokens, grad_w_query, grad_w_key, grad_w_value, grad_w_out)


def solution(mesh):
    in_specs = (
        P("seq", None),
        P("seq", None),
        P(None, "head"),
        P(None, "head"),
        P(None, "head"),
        P("head", None),
        P(),
    )
    out_specs = (
        P("seq", "head"),
        P("seq", "head"),
        P("seq", "head"),
        P("seq", "head"),
        P("seq", "head"),
        P("head", "seq"),
    )
    return jax.shard_map(body, mesh=mesh, in_specs=in_specs, out_specs=out_specs, check_vma=False)
```

```python
import functools
import math

import jax
import jax.numpy as jnp
import numpy as np
from jax import lax
from jax.experimental import pallas as pl
from jax.experimental.pallas import tpu as pltpu
from jax.sharding import PartitionSpec as P

DH = 128
LEAF = 128
LANES = 128

soft_cap = 6.0
noise_level = 0.5
prime_mod = 32749
inv_prime = 1.0 / prime_mod
BF = jnp.bfloat16
F32 = jnp.float32


def centre(residue):
    return jnp.where(residue > prime_mod // 2, residue - prime_mod, residue)


def dot32(left, right):
    return jnp.dot(left, right, preferred_element_type=F32)


def quotient(x, bias):
    return (x.astype(F32) * inv_prime - bias).astype(jnp.int32)


def perturb(axis_no, row_hash, row_base, col_hash, col_base, w_ref, out_ref):
    rows, cols = w_ref.shape
    chunk = min(rows, 256 if axis_no == 0 else 128)
    spread = None
    if axis_no == 0:

        def add_squares(i, total):
            part = w_ref[pl.ds(pl.multiple_of(i * chunk, chunk), chunk), :].astype(F32)
            return total + jnp.sum(part * part, axis=0, keepdims=True)

        squares = lax.fori_loop(0, rows // chunk, add_squares, jnp.zeros((1, cols), F32))
        spread = noise_level * jnp.sqrt(squares * (1.0 / rows) + 1e-06)

    def do_rows(i, carry):
        here = pl.ds(pl.multiple_of(i * chunk, chunk), chunk)
        r_hash = row_hash[here, :]
        r_id = lax.broadcasted_iota(jnp.int32, (chunk, LANES), 0) + (row_base + i * chunk)
        if axis_no == 0:
            base = spread
        else:
            whole = w_ref[here, :].astype(F32)
            mean = jnp.sum(whole * whole, axis=1, keepdims=True) * (1.0 / cols)
            base = noise_level * jnp.sqrt(mean + 1e-06)
        slope = base * (2.0 / (prime_mod - 1))
        for j in range(cols // LANES):
            at = slice(j * LANES, (j + 1) * LANES)
            c_id = lax.broadcasted_iota(jnp.int32, (1, LANES), 1) + (col_base + j * LANES)
            h = r_hash + col_hash[:, at]
            x = h * h + c_id
            h = x - quotient(x, 0.0) * prime_mod
            x = h * h + r_id
            h = x - quotient(x, 0.0078125) * prime_mod
            h = jnp.where(h >= prime_mod, h - prime_mod, h)
            step = slope[:, at] if axis_no == 0 else slope
            shift = base[:, at] if axis_no == 0 else base
            out_ref[here, at] = (w_ref[here, at].astype(F32) + (h.astype(F32) * step - shift)).astype(
                BF
            )
        return carry

    lax.fori_loop(0, rows // chunk, do_rows, 0)


def hash_rows(out_ref, row_base):
    rows = out_ref.shape[0]
    ids = lax.broadcasted_iota(jnp.int32, (rows, LANES), 0) + row_base
    x = ids * 7919
    out_ref[...] = centre(x - quotient(x, 0.0) * prime_mod)


def pair_mean(count):
    r = lax.broadcasted_iota(jnp.int32, (count // 2, count), 0)
    c = lax.broadcasted_iota(jnp.int32, (count // 2, count), 1)
    return jnp.where(c // 2 == r, 0.5, 0.0).astype(BF)


def coarse_levels(k_ref, v_ref, outs):
    cols = k_ref.shape[1]
    for n, src in enumerate((k_ref, v_ref)):
        rows = src[...]
        for out in outs:
            rows = dot32(pair_mean(rows.shape[0]), rows).astype(BF)
            out[:, n * cols : (n + 1) * cols] = rows


def attention_kernel(
    tok_rows,
    cross_rows,
    q_ref,
    k_ref,
    v_ref,
    do_ref,
    k1_ref,
    v1_ref,
    kx_ref,
    vx_ref,
    att_ref,
    dq_ref,
    dk_ref,
    dv_ref,
    dkvx_ref,
):
    pair = 2 * LEAF
    groups = tok_rows // pair
    scale_q = 1.0 / math.sqrt(DH)
    total_keys = pair + LEAF + cross_rows
    rows = lax.broadcasted_iota(jnp.int32, (total_keys, 1), 0)
    log_m = jnp.where(rows < pair, 0, (rows - pair) // LEAF + 1).astype(F32)
    dk1 = [None] * groups
    dv1 = [None] * groups
    dkx = None
    dvx = None
    for g in range(groups):
        own = slice(g * pair, (g + 1) * pair)
        other = slice((g ^ 1) * LEAF, ((g ^ 1) + 1) * LEAF)
        keys = jnp.concatenate([k_ref[own, :], k1_ref[other, :], kx_ref[...]], axis=0)
        values = jnp.concatenate([v_ref[own, :], v1_ref[other, :], vx_ref[...]], axis=0)
        q = q_ref[own, :]
        do = do_ref[own, :]
        do_t = do.astype(F32).T
        s = dot32(keys, q.astype(F32).T.astype(BF))
        t = jnp.tanh(s * (scale_q / soft_cap))
        w = jnp.exp2(t * (soft_cap * math.log2(math.e)) + log_m)
        weight_sum = jnp.sum(w, axis=0, keepdims=True)
        values_t = values.astype(F32).T.astype(BF)
        att_t = (dot32(values_t, w.astype(BF)) / weight_sum).astype(BF).astype(F32)
        att_ref[own, :] = att_t.T.astype(BF)
        delta = jnp.sum(att_t * do_t, axis=0, keepdims=True)
        p = w * (1.0 / weight_sum)
        dv = dot32(p.astype(BF), do)
        dp = dot32(values, do_t.astype(BF))
        grad = (p * (dp - delta) * (1.0 - t * t)).astype(BF)
        dk = dot32(grad, q) * scale_q
        keys_t = keys.astype(F32).T.astype(BF)
        dq_ref[own, :] = (dot32(keys_t, grad) * scale_q).T.astype(BF)
        dk_ref[own, :] = dk[:pair]
        dv_ref[own, :] = dv[:pair]
        dk1[g ^ 1] = dk[pair : pair + LEAF]
        dv1[g ^ 1] = dv[pair : pair + LEAF]
        dkx = dk[pair + LEAF :] if dkx is None else dkx + dk[pair + LEAF :]
        dvx = dv[pair + LEAF :] if dvx is None else dvx + dv[pair + LEAF :]
    r = lax.broadcasted_iota(jnp.int32, (pair, LEAF), 0)
    c = lax.broadcasted_iota(jnp.int32, (pair, LEAF), 1)
    expand = jnp.where(r // 2 == c, 0.5, 0.0).astype(BF)
    for g in range(groups):
        own = slice(g * pair, (g + 1) * pair)
        for ref, upper in ((dk_ref, dk1[g]), (dv_ref, dv1[g])):
            high = upper.astype(BF)
            low = (upper - high.astype(F32)).astype(BF)
            ref[own, :] += dot32(expand, high) + dot32(expand, low)
    dkvx_ref[0] = dkx.astype(BF)
    dkvx_ref[1] = dvx.astype(BF)


def fused_attention(q, k, v, do, kv1, kvx):
    tok_rows, cols = q.shape
    heads = cols // DH
    cross_rows = kvx.shape[0]

    def spec(rows, shift=0):
        return pl.BlockSpec((rows, DH), lambda h: (0, h + shift))

    out_shape = [
        jax.ShapeDtypeStruct((tok_rows, cols), BF),
        jax.ShapeDtypeStruct((tok_rows, cols), BF),
        jax.ShapeDtypeStruct((tok_rows, cols), F32),
        jax.ShapeDtypeStruct((tok_rows, cols), F32),
        jax.ShapeDtypeStruct((2, cross_rows, cols), BF),
    ]
    scores = tok_rows * (3 * LEAF + cross_rows) * heads
    return pl.pallas_call(
        functools.partial(attention_kernel, tok_rows, cross_rows),
        grid=(heads,),
        in_specs=[spec(tok_rows)] * 4
        + [spec(kv1.shape[0]), spec(kv1.shape[0], heads)]
        + [spec(cross_rows), spec(cross_rows, heads)],
        out_specs=[spec(tok_rows)] * 4
        + [pl.BlockSpec((2, cross_rows, DH), lambda h: (0, 0, h))],
        out_shape=out_shape,
        compiler_params=pltpu.CompilerParams(vmem_limit_bytes=48 << 20),
        cost_estimate=pl.CostEstimate(
            flops=12 * scores * DH, bytes_accessed=16 * tok_rows * cols, transcendentals=2 * scores
        ),
        name="attention",
    )(q, k, v, do, kv1, kv1, kvx, kvx)


def cross_rows_of(apart):
    return LEAF >> (apart.bit_length() - 1)


def upper_matrix(tok_rows, seq_count):
    parts = []
    for apart in range(1, seq_count):
        count = cross_rows_of(apart)
        wide = tok_rows // count
        parts.append(np.kron(np.eye(count), np.ones((wide, 1))) / wide)
    return jnp.asarray(np.concatenate(parts, axis=1), BF)


def flipped(idx, apart):
    peer = idx
    for bit in range(apart.bit_length()):
        if apart >> bit & 1:
            peer = peer + (1 << bit) * (1 - 2 * (idx // (1 << bit) % 2))
    return peer


def dot_nt(left, right):
    return lax.dot_general(left, right, (((1,), (1,)), ((), ())), preferred_element_type=F32)


def remote(src, dst, send_sem, recv_sem, axis, peer):
    return pltpu.make_async_remote_copy(
        src_ref=src,
        dst_ref=dst,
        send_sem=send_sem,
        recv_sem=recv_sem,
        device_id={axis: peer},
        device_id_type=pl.DeviceIdType.MESH,
    )


def greet(axis, peer):
    pl.semaphore_signal(
        pltpu.get_barrier_semaphore(),
        inc=1,
        device_id={axis: peer},
        device_id_type=pl.DeviceIdType.MESH,
    )


def front_kernel(
    seq_count,
    tokens_hbm,
    cot_hbm,
    wq_hbm,
    wk_hbm,
    wv_hbm,
    wo_hbm,
    hq_ref,
    hk_ref,
    hv_ref,
    ho_ref,
    wq_ref,
    wk_ref,
    wv_ref,
    wo_ref,
    q_ref,
    k_ref,
    v_ref,
    do_ref,
    kv1_ref,
    kvx_ref,
    tok_pair_ref,
    tokens,
    cot,
    w_in,
    wo_in,
    all_hash,
    own_hash,
    tok_send,
    coarse,
    load,
    send,
    recv,
):
    seq_idx = lax.axis_index("seq")
    head_idx = lax.axis_index("head")
    tok_rows = tokens.shape[0]
    head_cols = k_ref.shape[1]
    outer, _, share = tok_send.shape
    inner = seq_idx % 2
    loads = [
        pltpu.make_async_copy(src, dst, load.at[n])
        for n, (src, dst) in enumerate(
            (
                (tokens_hbm, tokens),
                (wk_hbm, w_in.at[0]),
                (wv_hbm, w_in.at[1]),
                (wq_hbm, w_in.at[2]),
                (wo_hbm, wo_in),
                (cot_hbm, cot),
            )
        )
    ]
    for copy in loads:
        copy.start()
    barrier = pltpu.get_barrier_semaphore()
    for apart in range(1, seq_count):
        greet("seq", flipped(seq_idx, apart))
    hash_rows(all_hash, 0)
    hash_rows(own_hash, head_idx * head_cols)
    loads[0].wait()
    for c in range(outer):
        low = tokens[:, 2 * c * share : (2 * c + 1) * share]
        high = tokens[:, (2 * c + 1) * share : (2 * c + 2) * share]
        tok_send[c] = jnp.where(inner == 0, high, low)
    pl.semaphore_wait(barrier, seq_count - 1)
    tok_copy = remote(
        tok_send, tok_pair_ref, send.at[0], recv.at[0], "seq", flipped(seq_idx, 1)
    )
    tok_copy.start()

    block = min(tok_rows, 128)

    def project(src, w_ref, out_ref, form):
        def rows_at(i, carry):
            here = pl.ds(pl.multiple_of(i * block, block), block)
            out_ref[here, :] = form(src[here, :], w_ref[...]).astype(BF)
            return carry

        lax.fori_loop(0, tok_rows // block, rows_at, 0)

    own_base = head_idx * head_cols
    loads[1].wait()
    perturb(0, all_hash, 0, hk_ref, own_base, w_in.at[0], wk_ref)
    project(tokens, wk_ref, k_ref, dot32)
    loads[2].wait()
    perturb(0, all_hash, 0, hv_ref, own_base, w_in.at[1], wv_ref)
    project(tokens, wv_ref, v_ref, dot32)
    coarse_levels(k_ref, v_ref, [kv1_ref] + list(coarse))
    copies = []
    at = 0
    for apart in range(1, seq_count):
        count = cross_rows_of(apart)
        copies.append(
            remote(
                coarse[apart.bit_length() - 1],
                kvx_ref.at[pl.ds(at, count), :],
                send.at[apart],
                recv.at[apart],
                "seq",
                flipped(seq_idx, apart),
            )
        )
        at += count
    for copy in copies:
        copy.start()
    loads[3].wait()
    perturb(0, all_hash, 0, hq_ref, own_base, w_in.at[2], wq_ref)
    project(tokens, wq_ref, q_ref, dot32)
    loads[4].wait()
    perturb(1, own_hash, own_base, ho_ref, 0, wo_in, wo_ref)
    loads[5].wait()
    project(cot, wo_ref, do_ref, dot_nt)
    for copy in copies + [tok_copy]:
        copy.wait()


def front(seq_count, tokens, cotangent, weights, hashes):
    tok_rows, model_width = tokens.shape
    head_cols = weights[0].shape[1]
    outer, share = seq_count // 2, model_width // seq_count
    bits = seq_count.bit_length() - 1
    vmem = pl.BlockSpec(memory_space=pltpu.VMEM)
    hbm = pl.BlockSpec(memory_space=pl.ANY)
    dma = pltpu.SemaphoreType.DMA

    def array(*shape):
        return jax.ShapeDtypeStruct(shape, BF)

    cross_rows = sum(cross_rows_of(d) for d in range(1, seq_count))
    return pl.pallas_call(
        functools.partial(front_kernel, seq_count),
        in_specs=[hbm] * 6 + [vmem] * 4,
        out_specs=[vmem] * 11,
        out_shape=[array(*w.shape) for w in weights]
        + [array(tok_rows, head_cols)] * 4
        + [array(tok_rows // 2, 2 * head_cols), array(cross_rows, 2 * head_cols)]
        + [array(outer, tok_rows, share)],
        scratch_shapes=[
            pltpu.VMEM(tokens.shape, BF),
            pltpu.VMEM(tokens.shape, BF),
            pltpu.VMEM((3,) + weights[0].shape, BF),
            pltpu.VMEM(weights[3].shape, BF),
            pltpu.VMEM((model_width, LANES), jnp.int32),
            pltpu.VMEM((head_cols, LANES), jnp.int32),
            pltpu.VMEM((outer, tok_rows, share), BF),
            [pltpu.VMEM((tok_rows >> n + 2, 2 * head_cols), BF) for n in range(bits)],
            dma((6,)),
            dma((seq_count,)),
            dma((seq_count,)),
        ],
        compiler_params=pltpu.CompilerParams(
            collective_id=1, has_side_effects=True, vmem_limit_bytes=56 << 20
        ),
        cost_estimate=pl.CostEstimate(
            flops=8 * tok_rows * model_width * head_cols,
            bytes_accessed=32 << 20,
            transcendentals=0,
        ),
        name="front",
    )(tokens, cotangent, *weights, *hashes)


def tail_kernel(
    seq_count,
    head_count,
    att_ref,
    dq_ref,
    dk_own_ref,
    dv_own_ref,
    dkvx_ref,
    upper_ref,
    tokens_ref,
    cot_ref,
    tok_pair_ref,
    wq_ref,
    wk_ref,
    wv_ref,
    wo_ref,
    attended_ref,
    grad_tok_ref,
    gq_ref,
    gk_ref,
    gv_ref,
    go_ref,
    grads,
    pairs,
    tok_t,
    cot_t,
    tok_pair_t,
    half_out,
    half_in,
    back_in,
    head_out,
    head_in,
    chain_out,
    up_in,
    down_in,
    pair_send,
    pair_recv,
    back_send,
    back_recv,
    head_send,
    head_recv,
    chain_send,
    up_recv,
    down_recv,
):
    seq_idx = lax.axis_index("seq")
    head_idx = lax.axis_index("head")
    outer = seq_count // 2
    z = seq_idx // 2
    inner = seq_idx % 2
    partner = flipped(seq_idx, 1)
    head_cols = att_ref.shape[1]

    outer_share = tok_pair_ref.shape[2]
    barrier = pltpu.get_barrier_semaphore()
    for apart in range(1, seq_count):
        greet("seq", flipped(seq_idx, apart))
    for apart in range(1, head_count):
        greet("head", (head_idx + apart) % head_count)
    pl.semaphore_wait(barrier, seq_count + head_count - 2)

    backs = []
    at = 0
    for apart in range(1, seq_count):
        rows = pl.ds(at, cross_rows_of(apart))
        at += cross_rows_of(apart)
        backs.append(
            remote(
                dkvx_ref.at[:, rows, :],
                back_in.at[:, rows, :],
                back_send.at[apart],
                back_recv.at[apart],
                "seq",
                flipped(seq_idx, apart),
            )
        )
    for copy in backs:
        copy.start()

    sources = (dq_ref, att_ref, grads.at[0], grads.at[1])
    outs = (gq_ref, go_ref, gk_ref, gv_ref)
    pair_copies = [
        remote(
            half_out if n == 1 else sources[n],
            half_in if n == 1 else pairs.at[n],
            pair_send.at[n],
            pair_recv.at[n],
            "seq",
            partner,
        )
        for n in range(4)
    ]
    pair_copies[0].start()

    def transpose_into(dst, src):
        width = min(256, src.shape[1])

        def columns(i, carry):
            here = pl.ds(pl.multiple_of(i * width, width), width)
            dst[here, :] = src[:, here].astype(F32).T.astype(BF)
            return carry

        lax.fori_loop(0, src.shape[1] // width, columns, 0)

    def own_rows(n, which):
        return pl.ds(pl.multiple_of((2 * n + which) * outer_share, outer_share), outer_share)

    def send_terms(which, term, result_ref):
        copies = []
        for apart in range(1, head_count):
            peer = (head_idx + apart) % head_count
            head_out[which, apart - 1] = term(peer).astype(BF)
            copy = remote(
                head_out.at[which, apart - 1],
                head_in.at[which, apart - 1],
                head_send.at[which, apart - 1],
                head_recv.at[which, apart - 1],
                "head",
                peer,
            )
            copy.start()
            copies.append(copy)
        return copies

    def finish_terms(which, term, copies, result_ref):
        total = term(head_idx)
        for apart, copy in enumerate(copies):
            copy.wait()
            total = total + head_in[which, apart].astype(F32)
        result_ref[...] = total.astype(BF)

    def piece(n):
        return pl.ds(pl.multiple_of(n * head_cols, head_cols), head_cols)

    def out_term(n):
        return dot32(att_ref[...], wo_ref[:, piece(n)])

    def in_term(n):
        return (
            dot_nt(dq_ref[...], wq_ref[piece(n), :])
            + dot_nt(grads[0], wk_ref[piece(n), :])
            + dot_nt(grads[1], wv_ref[piece(n), :])
        )

    def partial(n, c):
        if n == 1:
            return dot32(cot_t[own_rows(c, inner), :], att_ref[...]) + half_in[c].astype(F32)
        mine = dot32(tok_t[own_rows(c, inner), :], sources[n][...])
        return mine + dot32(tok_pair_t[c], pairs[n])

    def up_copy(n, c):
        return remote(
            chain_out.at[n, c], up_in.at[n, c], chain_send.at[n, c], up_recv.at[n, c],
            "seq", (seq_idx + 2) % seq_count,
        )

    def down_copy(n, c):
        return remote(
            chain_out.at[n, c], down_in.at[n, c], chain_send.at[n, c], down_recv.at[n, c],
            "seq", (seq_idx + seq_count - 2) % seq_count,
        )

    def chain(n):
        pair_copies[n].wait_recv()

        def step(t, carry):
            @pl.when(z <= t - 1)
            def _():
                c = z + outer - t
                chain_out[n, c] = partial(n, c).astype(BF)

                @pl.when(z > 0)
                def _():
                    up_copy(n, c).wait_recv()
                    chain_out[n, c] = (
                        chain_out[n, c].astype(F32) + up_in[n, c].astype(F32)
                    ).astype(BF)

                up_copy(n, c).start()

            @pl.when(z >= outer - t)
            def _():
                c = z + t - outer
                chain_out[n, c] = partial(n, c).astype(BF)

                @pl.when(z < outer - 1)
                def _():
                    down_copy(n, c).wait_recv()
                    chain_out[n, c] = (
                        chain_out[n, c].astype(F32) + down_in[n, c].astype(F32)
                    ).astype(BF)

                down_copy(n, c).start()

            return carry

        lax.fori_loop(1, outer, step, 0)

    def finish_chain(n):
        own = partial(n, z)

        def store(total):
            outs[n][...] = total.T if n == 1 else total

        @pl.when(z == 0)
        def _():
            down_copy(n, z).wait_recv()
            store(own + down_in[n, z].astype(F32))

        @pl.when(z == outer - 1)
        def _():
            up_copy(n, z).wait_recv()
            store(own + up_in[n, z].astype(F32))

        @pl.when((z > 0) & (z < outer - 1))
        def _():
            up_copy(n, z).wait_recv()
            down_copy(n, z).wait_recv()
            store(own + up_in[n, z].astype(F32) + down_in[n, z].astype(F32))

    att_copies = send_terms(0, out_term, attended_ref)
    transpose_into(tok_t, tokens_ref)

    def transpose_pair(c, carry):
        tok_pair_t[c] = tok_pair_ref[c].astype(F32).T.astype(BF)
        return carry

    lax.fori_loop(0, outer, transpose_pair, 0)
    for copy in backs:
        copy.wait_recv()
    grads[0] = (dk_own_ref[...] + dot32(upper_ref[...], back_in[0])).astype(BF)
    grads[1] = (dv_own_ref[...] + dot32(upper_ref[...], back_in[1])).astype(BF)
    pair_copies[2].start()
    pair_copies[3].start()
    chain(0)
    transpose_into(cot_t, cot_ref)

    def send_half(c, carry):
        half_out[c] = dot32(cot_t[own_rows(c, 1 - inner), :], att_ref[...]).astype(BF)
        return carry

    lax.fori_loop(0, outer, send_half, 0)
    pair_copies[1].start()
    tok_copies = send_terms(1, in_term, grad_tok_ref)
    chain(2)
    finish_chain(0)
    chain(3)
    finish_terms(0, out_term, att_copies, attended_ref)
    finish_chain(2)
    chain(1)
    finish_terms(1, in_term, tok_copies, grad_tok_ref)
    finish_chain(3)
    finish_chain(1)
    for copy in backs + pair_copies:
        copy.wait_send()

    def drain(c, carry):
        @pl.when(c != z)
        def _():
            for n in range(4):
                up_copy(n, c).wait_send()

        return carry

    lax.fori_loop(0, outer, drain, 0)


def tail(seq_count, head_count, *arrays):
    att, dkvx, tokens, tok_pair = arrays[0], arrays[4], arrays[6], arrays[8]
    tok_rows, head_cols = att.shape
    outer, _, share = tok_pair.shape
    vmem = pl.BlockSpec(memory_space=pltpu.VMEM)
    chunk = (4, outer, share, head_cols)
    grad = jax.ShapeDtypeStruct((share, head_cols), F32)
    tokens_out = jax.ShapeDtypeStruct((tok_rows, head_cols), BF)
    dma = pltpu.SemaphoreType.DMA
    return pl.pallas_call(
        functools.partial(tail_kernel, seq_count, head_count),
        in_specs=[vmem] * len(arrays),
        out_specs=[vmem] * 6,
        out_shape=[tokens_out] * 2
        + [grad] * 3
        + [jax.ShapeDtypeStruct((head_cols, share), F32)],
        scratch_shapes=[
            pltpu.VMEM((2, tok_rows, head_cols), BF),
            pltpu.VMEM((4, tok_rows, head_cols), BF),
            pltpu.VMEM(tokens.shape[::-1], BF),
            pltpu.VMEM(tokens.shape[::-1], BF),
            pltpu.VMEM((outer, share, tok_rows), BF),
            pltpu.VMEM((outer, share, head_cols), BF),
            pltpu.VMEM((outer, share, head_cols), BF),
            pltpu.VMEM(dkvx.shape, BF),
            pltpu.VMEM((2, head_count - 1, tok_rows, head_cols), BF),
            pltpu.VMEM((2, head_count - 1, tok_rows, head_cols), BF),
            pltpu.VMEM(chunk, BF),
            pltpu.VMEM(chunk, BF),
            pltpu.VMEM(chunk, BF),
            dma((4,)),
            dma((4,)),
            dma((seq_count,)),
            dma((seq_count,)),
            dma((2, head_count - 1)),
            dma((2, head_count - 1)),
            dma((4, outer)),
            dma((4, outer)),
            dma((4, outer)),
        ],
        compiler_params=pltpu.CompilerParams(
            collective_id=0, has_side_effects=True, vmem_limit_bytes=60 << 20
        ),
        cost_estimate=pl.CostEstimate(
            flops=20 * tok_rows * head_cols * share * outer,
            bytes_accessed=32 << 20,
            transcendentals=0,
        ),
        name="tail",
    )(*arrays)


def body(tokens, cotangent, w_query, w_key, w_value, w_out, seeds):
    seq_count = lax.axis_size("seq")
    head_count = lax.axis_size("head")
    head_idx = lax.axis_index("head")
    tok_rows, model_width = tokens.shape
    head_cols = w_query.shape[1]
    all_ids = jnp.arange(model_width, dtype=jnp.int32)
    own_ids = head_idx * head_cols + jnp.arange(head_cols, dtype=jnp.int32)

    def hash_cols(ids, seed):
        seeded = (ids * 10007 % prime_mod + seed * 31337 % prime_mod) % prime_mod
        return centre(seeded)[None, :]

    hashes = [hash_cols(own_ids, seeds[n]) for n in range(3)] + [hash_cols(all_ids, seeds[3])]
    (
        query_w,
        key_w,
        value_w,
        out_w,
        queries,
        keys,
        values,
        grad_att,
        kv1,
        kvx,
        tok_pair,
    ) = front(seq_count, tokens, cotangent, (w_query, w_key, w_value, w_out), hashes)
    att, dq, dk_own, dv_own, dkvx = fused_attention(queries, keys, values, grad_att, kv1, kvx)
    return tuple(
        tail(
            seq_count,
            head_count,
            att,
            dq,
            dk_own,
            dv_own,
            dkvx,
            upper_matrix(tok_rows, seq_count),
            tokens,
            cotangent,
            tok_pair,
            query_w,
            key_w,
            value_w,
            out_w,
        )
    )


def solution(mesh):
    in_specs = (
        P("seq", None),
        P("seq", None),
        P(None, "head"),
        P(None, "head"),
        P(None, "head"),
        P("head", None),
        P(),
    )
    out_specs = (
        P("seq", "head"),
        P("seq", "head"),
        P("seq", "head"),
        P("seq", "head"),
        P("seq", "head"),
        P("head", "seq"),
    )
    return jax.shard_map(body, mesh=mesh, in_specs=in_specs, out_specs=out_specs, check_vma=False)
```

```python
import functools
import math

import jax
import jax.numpy as jnp
import numpy as np
from jax import lax
from jax.experimental import pallas as pl
from jax.experimental.pallas import tpu as pltpu
from jax.sharding import PartitionSpec as P

DH = 128
LEAF = 128
LANES = 128

soft_cap = 6.0
noise_level = 0.5
prime_mod = 32749
inv_prime = 1.0 / prime_mod
BF = jnp.bfloat16
F32 = jnp.float32


def centre(residue):
    return jnp.where(residue > prime_mod // 2, residue - prime_mod, residue)


def dot32(left, right):
    return jnp.dot(left, right, preferred_element_type=F32)


def quotient(x, bias):
    return (x.astype(F32) * inv_prime - bias).astype(jnp.int32)


def perturb(axis_no, row_hash, row_base, col_hash, col_base, w_ref, out_ref):
    rows, cols = w_ref.shape
    chunk = min(rows, 256 if axis_no == 0 else 128)
    spread = None
    if axis_no == 0:

        def add_squares(i, total):
            part = w_ref[pl.ds(pl.multiple_of(i * chunk, chunk), chunk), :].astype(F32)
            return total + jnp.sum(part * part, axis=0, keepdims=True)

        squares = lax.fori_loop(0, rows // chunk, add_squares, jnp.zeros((1, cols), F32))
        spread = noise_level * jnp.sqrt(squares * (1.0 / rows) + 1e-06)

    def do_rows(i, carry):
        here = pl.ds(pl.multiple_of(i * chunk, chunk), chunk)
        r_hash = row_hash[here, :]
        r_id = lax.broadcasted_iota(jnp.int32, (chunk, LANES), 0) + (row_base + i * chunk)
        if axis_no == 0:
            base = spread
        else:
            whole = w_ref[here, :].astype(F32)
            mean = jnp.sum(whole * whole, axis=1, keepdims=True) * (1.0 / cols)
            base = noise_level * jnp.sqrt(mean + 1e-06)
        slope = base * (2.0 / (prime_mod - 1))
        for j in range(cols // LANES):
            at = slice(j * LANES, (j + 1) * LANES)
            c_id = lax.broadcasted_iota(jnp.int32, (1, LANES), 1) + (col_base + j * LANES)
            h = r_hash + col_hash[:, at]
            x = h * h + c_id
            h = x - quotient(x, 0.0) * prime_mod
            x = h * h + r_id
            h = x - quotient(x, 0.0078125) * prime_mod
            h = jnp.where(h >= prime_mod, h - prime_mod, h)
            step = slope[:, at] if axis_no == 0 else slope
            shift = base[:, at] if axis_no == 0 else base
            out_ref[here, at] = (w_ref[here, at].astype(F32) + (h.astype(F32) * step - shift)).astype(
                BF
            )
        return carry

    lax.fori_loop(0, rows // chunk, do_rows, 0)


def hash_rows(out_ref, row_base):
    rows = out_ref.shape[0]
    ids = lax.broadcasted_iota(jnp.int32, (rows, LANES), 0) + row_base
    x = ids * 7919
    out_ref[...] = centre(x - quotient(x, 0.0) * prime_mod)


def pair_mean(count):
    r = lax.broadcasted_iota(jnp.int32, (count // 2, count), 0)
    c = lax.broadcasted_iota(jnp.int32, (count // 2, count), 1)
    return jnp.where(c // 2 == r, 0.5, 0.0).astype(BF)


def coarse_levels(k_ref, v_ref, outs):
    cols = k_ref.shape[1]
    for n, src in enumerate((k_ref, v_ref)):
        rows = src[...]
        for out in outs:
            rows = dot32(pair_mean(rows.shape[0]), rows).astype(BF)
            out[:, n * cols : (n + 1) * cols] = rows


def attend(
    tok_rows,
    cross_rows,
    q_ref,
    k_ref,
    v_ref,
    do_ref,
    k1_ref,
    v1_ref,
    kx_ref,
    vx_ref,
    att_ref,
    dq_ref,
    dk_ref,
    dv_ref,
    dkvx_ref,
):
    pair = 2 * LEAF
    groups = tok_rows // pair
    scale_q = 1.0 / math.sqrt(DH)
    total_keys = pair + LEAF + cross_rows
    rows = lax.broadcasted_iota(jnp.int32, (total_keys, 1), 0)
    log_m = jnp.where(rows < pair, 0, (rows - pair) // LEAF + 1).astype(F32)
    dk1 = [None] * groups
    dv1 = [None] * groups
    dkx = None
    dvx = None
    for g in range(groups):
        own = slice(g * pair, (g + 1) * pair)
        other = slice((g ^ 1) * LEAF, ((g ^ 1) + 1) * LEAF)
        keys = jnp.concatenate([k_ref[own, :], k1_ref[other, :], kx_ref[...]], axis=0)
        values = jnp.concatenate([v_ref[own, :], v1_ref[other, :], vx_ref[...]], axis=0)
        q = q_ref[own, :]
        do = do_ref[own, :]
        do_t = do.astype(F32).T
        s = dot32(keys, q.astype(F32).T.astype(BF))
        t = jnp.tanh(s * (scale_q / soft_cap))
        w = jnp.exp2(t * (soft_cap * math.log2(math.e)) + log_m)
        weight_sum = jnp.sum(w, axis=0, keepdims=True)
        values_t = values.astype(F32).T.astype(BF)
        att_t = (dot32(values_t, w.astype(BF)) / weight_sum).astype(BF).astype(F32)
        att_ref[own, :] = att_t.T.astype(BF)
        delta = jnp.sum(att_t * do_t, axis=0, keepdims=True)
        p = w * (1.0 / weight_sum)
        dv = dot32(p.astype(BF), do)
        dp = dot32(values, do_t.astype(BF))
        grad = (p * (dp - delta) * (1.0 - t * t)).astype(BF)
        dk = dot32(grad, q) * scale_q
        keys_t = keys.astype(F32).T.astype(BF)
        dq_ref[own, :] = (dot32(keys_t, grad) * scale_q).T.astype(BF)
        dk_ref[own, :] = dk[:pair]
        dv_ref[own, :] = dv[:pair]
        dk1[g ^ 1] = dk[pair : pair + LEAF]
        dv1[g ^ 1] = dv[pair : pair + LEAF]
        dkx = dk[pair + LEAF :] if dkx is None else dkx + dk[pair + LEAF :]
        dvx = dv[pair + LEAF :] if dvx is None else dvx + dv[pair + LEAF :]
    r = lax.broadcasted_iota(jnp.int32, (pair, LEAF), 0)
    c = lax.broadcasted_iota(jnp.int32, (pair, LEAF), 1)
    expand = jnp.where(r // 2 == c, 0.5, 0.0).astype(BF)
    for g in range(groups):
        own = slice(g * pair, (g + 1) * pair)
        for ref, upper in ((dk_ref, dk1[g]), (dv_ref, dv1[g])):
            high = upper.astype(BF)
            low = (upper - high.astype(F32)).astype(BF)
            ref[own, :] += dot32(expand, high) + dot32(expand, low)
    dkvx_ref[0] = dkx.astype(BF)
    dkvx_ref[1] = dvx.astype(BF)


def cross_rows_of(apart):
    return LEAF >> (apart.bit_length() - 1)


def upper_matrix(tok_rows, seq_count):
    parts = []
    for apart in range(1, seq_count):
        count = cross_rows_of(apart)
        wide = tok_rows // count
        parts.append(np.kron(np.eye(count), np.ones((wide, 1))) / wide)
    return jnp.asarray(np.concatenate(parts, axis=1), BF)


def flipped(idx, apart):
    peer = idx
    for bit in range(apart.bit_length()):
        if apart >> bit & 1:
            peer = peer + (1 << bit) * (1 - 2 * (idx // (1 << bit) % 2))
    return peer


def dot_nt(left, right):
    return lax.dot_general(left, right, (((1,), (1,)), ((), ())), preferred_element_type=F32)


def remote(src, dst, send_sem, recv_sem, axis, peer):
    return pltpu.make_async_remote_copy(
        src_ref=src,
        dst_ref=dst,
        send_sem=send_sem,
        recv_sem=recv_sem,
        device_id={axis: peer},
        device_id_type=pl.DeviceIdType.MESH,
    )


def greet(axis, peer):
    pl.semaphore_signal(
        pltpu.get_barrier_semaphore(),
        inc=1,
        device_id={axis: peer},
        device_id_type=pl.DeviceIdType.MESH,
    )


def front_kernel(
    seq_count,
    tokens_hbm,
    cot_hbm,
    wq_hbm,
    wk_hbm,
    wv_hbm,
    wo_hbm,
    hq_ref,
    hk_ref,
    hv_ref,
    ho_ref,
    wq_ref,
    wk_ref,
    wv_ref,
    wo_ref,
    q_ref,
    k_ref,
    v_ref,
    do_ref,
    kv1_ref,
    kvx_ref,
    tok_pair_ref,
    tokens,
    cot,
    w_in,
    wo_in,
    all_hash,
    own_hash,
    tok_send,
    coarse,
    load,
    send,
    recv,
):
    seq_idx = lax.axis_index("seq")
    head_idx = lax.axis_index("head")
    tok_rows = tokens.shape[0]
    head_cols = k_ref.shape[1]
    outer, _, share = tok_send.shape
    inner = seq_idx % 2
    loads = [
        pltpu.make_async_copy(src, dst, load.at[n])
        for n, (src, dst) in enumerate(
            (
                (tokens_hbm, tokens),
                (wk_hbm, w_in.at[0]),
                (wv_hbm, w_in.at[1]),
                (wq_hbm, w_in.at[2]),
                (wo_hbm, wo_in),
                (cot_hbm, cot),
            )
        )
    ]
    for copy in loads:
        copy.start()
    barrier = pltpu.get_barrier_semaphore()
    for apart in range(1, seq_count):
        greet("seq", flipped(seq_idx, apart))
    hash_rows(all_hash, 0)
    hash_rows(own_hash, head_idx * head_cols)
    loads[0].wait()
    for c in range(outer):
        low = tokens[:, 2 * c * share : (2 * c + 1) * share]
        high = tokens[:, (2 * c + 1) * share : (2 * c + 2) * share]
        tok_send[c] = jnp.where(inner == 0, high, low)
    pl.semaphore_wait(barrier, seq_count - 1)
    tok_copy = remote(
        tok_send, tok_pair_ref, send.at[0], recv.at[0], "seq", flipped(seq_idx, 1)
    )
    tok_copy.start()

    block = min(tok_rows, 128)

    def project(src, w_ref, out_ref, form):
        def rows_at(i, carry):
            here = pl.ds(pl.multiple_of(i * block, block), block)
            out_ref[here, :] = form(src[here, :], w_ref[...]).astype(BF)
            return carry

        lax.fori_loop(0, tok_rows // block, rows_at, 0)

    own_base = head_idx * head_cols
    loads[1].wait()
    perturb(0, all_hash, 0, hk_ref, own_base, w_in.at[0], wk_ref)
    project(tokens, wk_ref, k_ref, dot32)
    loads[2].wait()
    perturb(0, all_hash, 0, hv_ref, own_base, w_in.at[1], wv_ref)
    project(tokens, wv_ref, v_ref, dot32)
    coarse_levels(k_ref, v_ref, [kv1_ref] + list(coarse))
    copies = []
    at = 0
    for apart in range(1, seq_count):
        count = cross_rows_of(apart)
        copies.append(
            remote(
                coarse[apart.bit_length() - 1],
                kvx_ref.at[pl.ds(at, count), :],
                send.at[apart],
                recv.at[apart],
                "seq",
                flipped(seq_idx, apart),
            )
        )
        at += count
    for copy in copies:
        copy.start()
    loads[3].wait()
    perturb(0, all_hash, 0, hq_ref, own_base, w_in.at[2], wq_ref)
    project(tokens, wq_ref, q_ref, dot32)
    loads[4].wait()
    perturb(1, own_hash, own_base, ho_ref, 0, wo_in, wo_ref)
    loads[5].wait()
    project(cot, wo_ref, do_ref, dot_nt)
    for copy in copies + [tok_copy]:
        copy.wait()


def front(seq_count, tokens, cotangent, weights, hashes):
    tok_rows, model_width = tokens.shape
    head_cols = weights[0].shape[1]
    outer, share = seq_count // 2, model_width // seq_count
    bits = seq_count.bit_length() - 1
    vmem = pl.BlockSpec(memory_space=pltpu.VMEM)
    hbm = pl.BlockSpec(memory_space=pl.ANY)
    dma = pltpu.SemaphoreType.DMA

    def array(*shape):
        return jax.ShapeDtypeStruct(shape, BF)

    cross_rows = sum(cross_rows_of(d) for d in range(1, seq_count))
    return pl.pallas_call(
        functools.partial(front_kernel, seq_count),
        in_specs=[hbm] * 6 + [vmem] * 4,
        out_specs=[vmem] * 11,
        out_shape=[array(*w.shape) for w in weights]
        + [array(tok_rows, head_cols)] * 4
        + [array(tok_rows // 2, 2 * head_cols), array(cross_rows, 2 * head_cols)]
        + [array(outer, tok_rows, share)],
        scratch_shapes=[
            pltpu.VMEM(tokens.shape, BF),
            pltpu.VMEM(tokens.shape, BF),
            pltpu.VMEM((3,) + weights[0].shape, BF),
            pltpu.VMEM(weights[3].shape, BF),
            pltpu.VMEM((model_width, LANES), jnp.int32),
            pltpu.VMEM((head_cols, LANES), jnp.int32),
            pltpu.VMEM((outer, tok_rows, share), BF),
            [pltpu.VMEM((tok_rows >> n + 2, 2 * head_cols), BF) for n in range(bits)],
            dma((6,)),
            dma((seq_count,)),
            dma((seq_count,)),
        ],
        compiler_params=pltpu.CompilerParams(
            collective_id=1, has_side_effects=True, vmem_limit_bytes=56 << 20
        ),
        cost_estimate=pl.CostEstimate(
            flops=8 * tok_rows * model_width * head_cols,
            bytes_accessed=32 << 20,
            transcendentals=0,
        ),
        name="front",
    )(tokens, cotangent, *weights, *hashes)


def tail_kernel(
    seq_count,
    head_count,
    q_ref,
    k_ref,
    v_ref,
    do_ref,
    kv1_ref,
    kvx_ref,
    upper_ref,
    tokens_ref,
    cot_ref,
    tok_pair_ref,
    wq_ref,
    wk_ref,
    wv_ref,
    wo_ref,
    attended_ref,
    grad_tok_ref,
    gq_ref,
    gk_ref,
    gv_ref,
    go_ref,
    att_ref,
    dq_ref,
    dk_own_ref,
    dv_own_ref,
    dkvx_ref,
    grads,
    pairs,
    tok_t,
    cot_t,
    tok_pair_t,
    half_out,
    half_in,
    back_in,
    head_out,
    head_in,
    chain_out,
    up_in,
    down_in,
    pair_send,
    pair_recv,
    dq_send,
    dq_recv,
    back_send,
    back_recv,
    head_send,
    head_recv,
    chain_send,
    up_recv,
    down_recv,
):
    seq_idx = lax.axis_index("seq")
    head_idx = lax.axis_index("head")
    outer = seq_count // 2
    z = seq_idx // 2
    inner = seq_idx % 2
    partner = flipped(seq_idx, 1)
    head_cols = att_ref.shape[1]

    outer_share = tok_pair_ref.shape[2]
    barrier = pltpu.get_barrier_semaphore()
    for apart in range(1, seq_count):
        greet("seq", flipped(seq_idx, apart))
    for apart in range(1, head_count):
        greet("head", (head_idx + apart) % head_count)
    pl.semaphore_wait(barrier, seq_count + head_count - 2)

    heads = head_cols // DH

    def head_columns(h, shift=0):
        return pl.ds(pl.multiple_of(h * DH + shift, DH), DH)

    def head_copies(h):
        cols = head_columns(h)
        copies = []
        at = 0
        for apart in range(1, seq_count):
            rows = pl.ds(at, cross_rows_of(apart))
            at += cross_rows_of(apart)
            copies.append(
                remote(
                    dkvx_ref.at[:, rows, cols],
                    back_in.at[:, rows, cols],
                    back_send.at[h, apart],
                    back_recv.at[h, apart],
                    "seq",
                    flipped(seq_idx, apart),
                )
            )
        copies.append(
            remote(
                dq_ref.at[:, cols],
                pairs.at[0, :, cols],
                dq_send.at[h],
                dq_recv.at[h],
                "seq",
                partner,
            )
        )
        return copies

    def one_head(h, carry):
        cols = head_columns(h)
        cross_cols = head_columns(h, head_cols)
        attend(
            q_ref.shape[0],
            kvx_ref.shape[0],
            q_ref.at[:, cols],
            k_ref.at[:, cols],
            v_ref.at[:, cols],
            do_ref.at[:, cols],
            kv1_ref.at[:, cols],
            kv1_ref.at[:, cross_cols],
            kvx_ref.at[:, cols],
            kvx_ref.at[:, cross_cols],
            att_ref.at[:, cols],
            dq_ref.at[:, cols],
            dk_own_ref.at[:, cols],
            dv_own_ref.at[:, cols],
            dkvx_ref.at[:, :, cols],
        )
        for copy in head_copies(h):
            copy.start()
        return carry

    sources = (dq_ref, att_ref, grads.at[0], grads.at[1])
    outs = (gq_ref, go_ref, gk_ref, gv_ref)
    pair_copies = [None] + [
        remote(
            half_out if n == 1 else sources[n],
            half_in if n == 1 else pairs.at[n],
            pair_send.at[n],
            pair_recv.at[n],
            "seq",
            partner,
        )
        for n in range(1, 4)
    ]

    def transpose_into(dst, src):
        width = min(256, src.shape[1])

        def columns(i, carry):
            here = pl.ds(pl.multiple_of(i * width, width), width)
            dst[here, :] = src[:, here].astype(F32).T.astype(BF)
            return carry

        lax.fori_loop(0, src.shape[1] // width, columns, 0)

    def own_rows(n, which):
        return pl.ds(pl.multiple_of((2 * n + which) * outer_share, outer_share), outer_share)

    def send_terms(which, term, result_ref):
        copies = []
        for apart in range(1, head_count):
            peer = (head_idx + apart) % head_count
            head_out[which, apart - 1] = term(peer).astype(BF)
            copy = remote(
                head_out.at[which, apart - 1],
                head_in.at[which, apart - 1],
                head_send.at[which, apart - 1],
                head_recv.at[which, apart - 1],
                "head",
                peer,
            )
            copy.start()
            copies.append(copy)
        return copies

    def finish_terms(which, term, copies, result_ref):
        total = term(head_idx)
        for apart, copy in enumerate(copies):
            copy.wait()
            total = total + head_in[which, apart].astype(F32)
        result_ref[...] = total.astype(BF)

    def piece(n):
        return pl.ds(pl.multiple_of(n * head_cols, head_cols), head_cols)

    def out_term(n):
        return dot32(att_ref[...], wo_ref[:, piece(n)])

    def in_term(n):
        return (
            dot_nt(dq_ref[...], wq_ref[piece(n), :])
            + dot_nt(grads[0], wk_ref[piece(n), :])
            + dot_nt(grads[1], wv_ref[piece(n), :])
        )

    def partial(n, c):
        if n == 1:
            return dot32(cot_t[own_rows(c, inner), :], att_ref[...]) + half_in[c].astype(F32)
        mine = dot32(tok_t[own_rows(c, inner), :], sources[n][...])
        return mine + dot32(tok_pair_t[c], pairs[n])

    def up_copy(n, c):
        return remote(
            chain_out.at[n, c], up_in.at[n, c], chain_send.at[n, c], up_recv.at[n, c],
            "seq", (seq_idx + 2) % seq_count,
        )

    def down_copy(n, c):
        return remote(
            chain_out.at[n, c], down_in.at[n, c], chain_send.at[n, c], down_recv.at[n, c],
            "seq", (seq_idx + seq_count - 2) % seq_count,
        )

    def chain(n):
        if n > 0:
            pair_copies[n].wait_recv()

        def step(t, carry):
            @pl.when(z <= t - 1)
            def _():
                c = z + outer - t
                chain_out[n, c] = partial(n, c).astype(BF)

                @pl.when(z > 0)
                def _():
                    up_copy(n, c).wait_recv()
                    chain_out[n, c] = (
                        chain_out[n, c].astype(F32) + up_in[n, c].astype(F32)
                    ).astype(BF)

                up_copy(n, c).start()

            @pl.when(z >= outer - t)
            def _():
                c = z + t - outer
                chain_out[n, c] = partial(n, c).astype(BF)

                @pl.when(z < outer - 1)
                def _():
                    down_copy(n, c).wait_recv()
                    chain_out[n, c] = (
                        chain_out[n, c].astype(F32) + down_in[n, c].astype(F32)
                    ).astype(BF)

                down_copy(n, c).start()

            return carry

        lax.fori_loop(1, outer, step, 0)

    def finish_chain(n):
        own = partial(n, z)

        def store(total):
            outs[n][...] = total.T if n == 1 else total

        @pl.when(z == 0)
        def _():
            down_copy(n, z).wait_recv()
            store(own + down_in[n, z].astype(F32))

        @pl.when(z == outer - 1)
        def _():
            up_copy(n, z).wait_recv()
            store(own + up_in[n, z].astype(F32))

        @pl.when((z > 0) & (z < outer - 1))
        def _():
            up_copy(n, z).wait_recv()
            down_copy(n, z).wait_recv()
            store(own + up_in[n, z].astype(F32) + down_in[n, z].astype(F32))

    lax.fori_loop(0, heads, one_head, 0)
    transpose_into(tok_t, tokens_ref)

    def transpose_pair(c, carry):
        tok_pair_t[c] = tok_pair_ref[c].astype(F32).T.astype(BF)
        return carry

    lax.fori_loop(0, outer, transpose_pair, 0)

    def head_arrived(h, carry):
        for copy in head_copies(h):
            copy.wait_recv()
        return carry

    lax.fori_loop(0, heads, head_arrived, 0)
    grads[0] = (dk_own_ref[...] + dot32(upper_ref[...], back_in[0])).astype(BF)
    pair_copies[2].start()
    grads[1] = (dv_own_ref[...] + dot32(upper_ref[...], back_in[1])).astype(BF)
    pair_copies[3].start()
    chain(0)
    att_copies = send_terms(0, out_term, attended_ref)
    transpose_into(cot_t, cot_ref)

    def send_half(c, carry):
        half_out[c] = dot32(cot_t[own_rows(c, 1 - inner), :], att_ref[...]).astype(BF)
        return carry

    lax.fori_loop(0, outer, send_half, 0)
    pair_copies[1].start()
    tok_copies = send_terms(1, in_term, grad_tok_ref)
    chain(2)
    finish_chain(0)
    chain(3)
    finish_terms(0, out_term, att_copies, attended_ref)
    finish_chain(2)
    chain(1)
    finish_terms(1, in_term, tok_copies, grad_tok_ref)
    finish_chain(3)
    finish_chain(1)
    for copy in pair_copies[1:]:
        copy.wait_send()

    def head_sent(h, carry):
        for copy in head_copies(h):
            copy.wait_send()
        return carry

    lax.fori_loop(0, heads, head_sent, 0)

    def drain(c, carry):
        @pl.when(c != z)
        def _():
            for n in range(4):
                up_copy(n, c).wait_send()

        return carry

    lax.fori_loop(0, outer, drain, 0)


def tail(seq_count, head_count, *arrays):
    queries, kvx, tokens, tok_pair = arrays[0], arrays[5], arrays[7], arrays[9]
    tok_rows, head_cols = queries.shape
    cross = (2, kvx.shape[0], head_cols)
    heads = head_cols // DH
    outer, _, share = tok_pair.shape
    vmem = pl.BlockSpec(memory_space=pltpu.VMEM)
    chunk = (4, outer, share, head_cols)
    grad = jax.ShapeDtypeStruct((share, head_cols), F32)
    tokens_out = jax.ShapeDtypeStruct((tok_rows, head_cols), BF)
    dma = pltpu.SemaphoreType.DMA
    return pl.pallas_call(
        functools.partial(tail_kernel, seq_count, head_count),
        in_specs=[vmem] * len(arrays),
        out_specs=[vmem] * 6,
        out_shape=[tokens_out] * 2
        + [grad] * 3
        + [jax.ShapeDtypeStruct((head_cols, share), F32)],
        scratch_shapes=[
            pltpu.VMEM((tok_rows, head_cols), BF),
            pltpu.VMEM((tok_rows, head_cols), BF),
            pltpu.VMEM((tok_rows, head_cols), F32),
            pltpu.VMEM((tok_rows, head_cols), F32),
            pltpu.VMEM(cross, BF),
            pltpu.VMEM((2, tok_rows, head_cols), BF),
            pltpu.VMEM((4, tok_rows, head_cols), BF),
            pltpu.VMEM(tokens.shape[::-1], BF),
            pltpu.VMEM(tokens.shape[::-1], BF),
            pltpu.VMEM((outer, share, tok_rows), BF),
            pltpu.VMEM((outer, share, head_cols), BF),
            pltpu.VMEM((outer, share, head_cols), BF),
            pltpu.VMEM(cross, BF),
            pltpu.VMEM((2, head_count - 1, tok_rows, head_cols), BF),
            pltpu.VMEM((2, head_count - 1, tok_rows, head_cols), BF),
            pltpu.VMEM(chunk, BF),
            pltpu.VMEM(chunk, BF),
            pltpu.VMEM(chunk, BF),
            dma((4,)),
            dma((4,)),
            dma((heads,)),
            dma((heads,)),
            dma((heads, seq_count)),
            dma((heads, seq_count)),
            dma((2, head_count - 1)),
            dma((2, head_count - 1)),
            dma((4, outer)),
            dma((4, outer)),
            dma((4, outer)),
        ],
        compiler_params=pltpu.CompilerParams(
            collective_id=0, has_side_effects=True, vmem_limit_bytes=60 << 20
        ),
        cost_estimate=pl.CostEstimate(
            flops=20 * tok_rows * head_cols * share * outer,
            bytes_accessed=32 << 20,
            transcendentals=0,
        ),
        name="tail",
    )(*arrays)


def settle_kernel(*refs):
    count = len(refs) // 2
    copies = [
        pltpu.make_async_copy(refs[n], refs[count + n], refs[-1].at[n]) for n in range(count)
    ]
    for copy in copies:
        copy.start()
    for copy in copies:
        copy.wait()


def settle(arrays):
    hbm = pl.BlockSpec(memory_space=pl.ANY)
    return pl.pallas_call(
        settle_kernel,
        in_specs=[hbm] * len(arrays),
        out_specs=[hbm] * len(arrays),
        out_shape=[jax.ShapeDtypeStruct(a.shape, a.dtype) for a in arrays],
        scratch_shapes=[pltpu.SemaphoreType.DMA((len(arrays),))],
        name="settle",
    )(*arrays)


def body(tokens, cotangent, w_query, w_key, w_value, w_out, seeds):
    seq_count = lax.axis_size("seq")
    head_count = lax.axis_size("head")
    head_idx = lax.axis_index("head")
    tok_rows, model_width = tokens.shape
    head_cols = w_query.shape[1]
    all_ids = jnp.arange(model_width, dtype=jnp.int32)
    own_ids = head_idx * head_cols + jnp.arange(head_cols, dtype=jnp.int32)

    def hash_cols(ids, seed):
        seeded = (ids * 10007 % prime_mod + seed * 31337 % prime_mod) % prime_mod
        return centre(seeded)[None, :]

    hashes = [hash_cols(own_ids, seeds[n]) for n in range(3)] + [hash_cols(all_ids, seeds[3])]
    (
        query_w,
        key_w,
        value_w,
        out_w,
        queries,
        keys,
        values,
        grad_att,
        kv1,
        kvx,
        tok_pair,
    ) = front(seq_count, tokens, cotangent, (w_query, w_key, w_value, w_out), hashes)
    return tuple(
        settle(
            tail(
                seq_count,
                head_count,
                queries,
                keys,
                values,
                grad_att,
                kv1,
                kvx,
                upper_matrix(tok_rows, seq_count),
                tokens,
                cotangent,
                tok_pair,
                query_w,
                key_w,
                value_w,
                out_w,
            )
        )
    )


def solution(mesh):
    in_specs = (
        P("seq", None),
        P("seq", None),
        P(None, "head"),
        P(None, "head"),
        P(None, "head"),
        P("head", None),
        P(),
    )
    out_specs = (
        P("seq", "head"),
        P("seq", "head"),
        P("seq", "head"),
        P("seq", "head"),
        P("seq", "head"),
        P("head", "seq"),
    )
    return jax.shard_map(body, mesh=mesh, in_specs=in_specs, out_specs=out_specs, check_vma=False)
```

```python
import functools
import math

import jax
import jax.numpy as jnp
import numpy as np
from jax import lax
from jax.experimental import pallas as pl
from jax.experimental.pallas import tpu as pltpu
from jax.sharding import PartitionSpec as P

DH = 128
LEAF = 128
LANES = 128

soft_cap = 6.0
noise_level = 0.5
prime_mod = 32749
inv_prime = 1.0 / prime_mod
BF = jnp.bfloat16
F32 = jnp.float32


def centre(residue):
    return jnp.where(residue > prime_mod // 2, residue - prime_mod, residue)


def dot32(left, right):
    return jnp.dot(left, right, preferred_element_type=F32)


def quotient(x, bias):
    return (x.astype(F32) * inv_prime - bias).astype(jnp.int32)


def perturb(axis_no, row_hash, row_base, col_hash, col_base, w_ref, out_ref):
    rows, cols = w_ref.shape
    chunk = min(rows, 256 if axis_no == 0 else 128)
    spread = None
    if axis_no == 0:

        def add_squares(i, total):
            part = w_ref[pl.ds(pl.multiple_of(i * chunk, chunk), chunk), :].astype(F32)
            return total + jnp.sum(part * part, axis=0, keepdims=True)

        squares = lax.fori_loop(0, rows // chunk, add_squares, jnp.zeros((1, cols), F32))
        spread = noise_level * jnp.sqrt(squares * (1.0 / rows) + 1e-06)

    def do_rows(i, carry):
        here = pl.ds(pl.multiple_of(i * chunk, chunk), chunk)
        r_hash = row_hash[here, :]
        r_id = lax.broadcasted_iota(jnp.int32, (chunk, LANES), 0) + (row_base + i * chunk)
        if axis_no == 0:
            base = spread
        else:
            whole = w_ref[here, :].astype(F32)
            mean = jnp.sum(whole * whole, axis=1, keepdims=True) * (1.0 / cols)
            base = noise_level * jnp.sqrt(mean + 1e-06)
        slope = base * (2.0 / (prime_mod - 1))
        for j in range(cols // LANES):
            at = slice(j * LANES, (j + 1) * LANES)
            c_id = lax.broadcasted_iota(jnp.int32, (1, LANES), 1) + (col_base + j * LANES)
            h = r_hash + col_hash[:, at]
            x = h * h + c_id
            h = x - quotient(x, 0.0) * prime_mod
            x = h * h + r_id
            h = x - quotient(x, 0.0078125) * prime_mod
            h = jnp.where(h >= prime_mod, h - prime_mod, h)
            step = slope[:, at] if axis_no == 0 else slope
            shift = base[:, at] if axis_no == 0 else base
            out_ref[here, at] = (w_ref[here, at].astype(F32) + (h.astype(F32) * step - shift)).astype(
                BF
            )
        return carry

    lax.fori_loop(0, rows // chunk, do_rows, 0)


def hash_rows(out_ref, row_base):
    rows = out_ref.shape[0]
    ids = lax.broadcasted_iota(jnp.int32, (rows, LANES), 0) + row_base
    x = ids * 7919
    out_ref[...] = centre(x - quotient(x, 0.0) * prime_mod)


def pair_mean(count):
    r = lax.broadcasted_iota(jnp.int32, (count // 2, count), 0)
    c = lax.broadcasted_iota(jnp.int32, (count // 2, count), 1)
    return jnp.where(c // 2 == r, 0.5, 0.0).astype(BF)


def coarse_levels(k_ref, v_ref, outs):
    cols = k_ref.shape[1]
    for n, src in enumerate((k_ref, v_ref)):
        rows = src[...]
        for out in outs:
            rows = dot32(pair_mean(rows.shape[0]), rows).astype(BF)
            out[:, n * cols : (n + 1) * cols] = rows


def attend(
    tok_rows,
    cross_rows,
    q_ref,
    k_ref,
    v_ref,
    do_ref,
    k1_ref,
    v1_ref,
    kx_ref,
    vx_ref,
    att_ref,
    dq_ref,
    dk_ref,
    dv_ref,
    dkvx_ref,
):
    pair = 2 * LEAF
    groups = tok_rows // pair
    scale_q = 1.0 / math.sqrt(DH)
    total_keys = pair + LEAF + cross_rows
    rows = lax.broadcasted_iota(jnp.int32, (total_keys, 1), 0)
    log_m = jnp.where(rows < pair, 0, (rows - pair) // LEAF + 1).astype(F32)
    dk1 = [None] * groups
    dv1 = [None] * groups
    dkx = None
    dvx = None
    for g in range(groups):
        own = slice(g * pair, (g + 1) * pair)
        other = slice((g ^ 1) * LEAF, ((g ^ 1) + 1) * LEAF)
        keys = jnp.concatenate([k_ref[own, :], k1_ref[other, :], kx_ref[...]], axis=0)
        values = jnp.concatenate([v_ref[own, :], v1_ref[other, :], vx_ref[...]], axis=0)
        q = q_ref[own, :]
        do = do_ref[own, :]
        do_t = do.astype(F32).T
        s = dot32(keys, q.astype(F32).T.astype(BF))
        t = jnp.tanh(s * (scale_q / soft_cap))
        w = jnp.exp2(t * (soft_cap * math.log2(math.e)) + log_m)
        weight_sum = jnp.sum(w, axis=0, keepdims=True)
        values_t = values.astype(F32).T.astype(BF)
        att_t = (dot32(values_t, w.astype(BF)) / weight_sum).astype(BF).astype(F32)
        att_ref[own, :] = att_t.T.astype(BF)
        delta = jnp.sum(att_t * do_t, axis=0, keepdims=True)
        p = w * (1.0 / weight_sum)
        dv = dot32(p.astype(BF), do)
        dp = dot32(values, do_t.astype(BF))
        grad = (p * (dp - delta) * (1.0 - t * t)).astype(BF)
        dk = dot32(grad, q) * scale_q
        keys_t = keys.astype(F32).T.astype(BF)
        dq_ref[own, :] = (dot32(keys_t, grad) * scale_q).T.astype(BF)
        dk_ref[own, :] = dk[:pair]
        dv_ref[own, :] = dv[:pair]
        dk1[g ^ 1] = dk[pair : pair + LEAF]
        dv1[g ^ 1] = dv[pair : pair + LEAF]
        dkx = dk[pair + LEAF :] if dkx is None else dkx + dk[pair + LEAF :]
        dvx = dv[pair + LEAF :] if dvx is None else dvx + dv[pair + LEAF :]
    r = lax.broadcasted_iota(jnp.int32, (pair, LEAF), 0)
    c = lax.broadcasted_iota(jnp.int32, (pair, LEAF), 1)
    expand = jnp.where(r // 2 == c, 0.5, 0.0).astype(BF)
    for g in range(groups):
        own = slice(g * pair, (g + 1) * pair)
        for ref, upper in ((dk_ref, dk1[g]), (dv_ref, dv1[g])):
            high = upper.astype(BF)
            low = (upper - high.astype(F32)).astype(BF)
            ref[own, :] += dot32(expand, high) + dot32(expand, low)
    dkvx_ref[0] = dkx.astype(BF)
    dkvx_ref[1] = dvx.astype(BF)


def cross_rows_of(apart):
    return LEAF >> (apart.bit_length() - 1)


def upper_matrix(tok_rows, seq_count):
    parts = []
    for apart in range(1, seq_count):
        count = cross_rows_of(apart)
        wide = tok_rows // count
        parts.append(np.kron(np.eye(count), np.ones((wide, 1))) / wide)
    return jnp.asarray(np.concatenate(parts, axis=1), BF)


def flipped(idx, apart):
    peer = idx
    for bit in range(apart.bit_length()):
        if apart >> bit & 1:
            peer = peer + (1 << bit) * (1 - 2 * (idx // (1 << bit) % 2))
    return peer


def dot_nt(left, right):
    return lax.dot_general(left, right, (((1,), (1,)), ((), ())), preferred_element_type=F32)


def remote(src, dst, send_sem, recv_sem, axis, peer):
    return pltpu.make_async_remote_copy(
        src_ref=src,
        dst_ref=dst,
        send_sem=send_sem,
        recv_sem=recv_sem,
        device_id={axis: peer},
        device_id_type=pl.DeviceIdType.MESH,
    )


def greet(axis, peer):
    pl.semaphore_signal(
        pltpu.get_barrier_semaphore(),
        inc=1,
        device_id={axis: peer},
        device_id_type=pl.DeviceIdType.MESH,
    )


def front_kernel(
    seq_count,
    tokens_hbm,
    cot_hbm,
    wq_hbm,
    wk_hbm,
    wv_hbm,
    wo_hbm,
    hq_ref,
    hk_ref,
    hv_ref,
    ho_ref,
    wq_ref,
    wk_ref,
    wv_ref,
    wo_ref,
    q_ref,
    k_ref,
    v_ref,
    do_ref,
    kv1_ref,
    kvx_ref,
    tok_pair_ref,
    tokens,
    cot,
    w_in,
    wo_in,
    all_hash,
    own_hash,
    tok_send,
    coarse,
    load,
    send,
    recv,
):
    seq_idx = lax.axis_index("seq")
    head_idx = lax.axis_index("head")
    tok_rows = tokens.shape[0]
    head_cols = k_ref.shape[1]
    outer, _, share = tok_send.shape
    inner = seq_idx % 2
    loads = [
        pltpu.make_async_copy(src, dst, load.at[n])
        for n, (src, dst) in enumerate(
            (
                (tokens_hbm, tokens),
                (wk_hbm, w_in.at[0]),
                (wv_hbm, w_in.at[1]),
                (wq_hbm, w_in.at[2]),
                (wo_hbm, wo_in),
                (cot_hbm, cot),
            )
        )
    ]
    for copy in loads:
        copy.start()
    barrier = pltpu.get_barrier_semaphore()
    for apart in range(1, seq_count):
        greet("seq", flipped(seq_idx, apart))
    hash_rows(all_hash, 0)
    hash_rows(own_hash, head_idx * head_cols)
    loads[0].wait()
    for c in range(outer):
        low = tokens[:, 2 * c * share : (2 * c + 1) * share]
        high = tokens[:, (2 * c + 1) * share : (2 * c + 2) * share]
        tok_send[c] = jnp.where(inner == 0, high, low)
    pl.semaphore_wait(barrier, seq_count - 1)
    tok_copy = remote(
        tok_send, tok_pair_ref, send.at[0], recv.at[0], "seq", flipped(seq_idx, 1)
    )
    tok_copy.start()

    block = min(tok_rows, 128)

    def project(src, w_ref, out_ref, form):
        def rows_at(i, carry):
            here = pl.ds(pl.multiple_of(i * block, block), block)
            out_ref[here, :] = form(src[here, :], w_ref[...]).astype(BF)
            return carry

        lax.fori_loop(0, tok_rows // block, rows_at, 0)

    own_base = head_idx * head_cols
    loads[1].wait()
    perturb(0, all_hash, 0, hk_ref, own_base, w_in.at[0], wk_ref)
    project(tokens, wk_ref, k_ref, dot32)
    loads[2].wait()
    perturb(0, all_hash, 0, hv_ref, own_base, w_in.at[1], wv_ref)
    project(tokens, wv_ref, v_ref, dot32)
    coarse_levels(k_ref, v_ref, [kv1_ref] + list(coarse))
    copies = []
    at = 0
    for apart in range(1, seq_count):
        count = cross_rows_of(apart)
        copies.append(
            remote(
                coarse[apart.bit_length() - 1],
                kvx_ref.at[pl.ds(at, count), :],
                send.at[apart],
                recv.at[apart],
                "seq",
                flipped(seq_idx, apart),
            )
        )
        at += count
    for copy in copies:
        copy.start()
    loads[3].wait()
    perturb(0, all_hash, 0, hq_ref, own_base, w_in.at[2], wq_ref)
    project(tokens, wq_ref, q_ref, dot32)
    loads[4].wait()
    perturb(1, own_hash, own_base, ho_ref, 0, wo_in, wo_ref)
    loads[5].wait()
    project(cot, wo_ref, do_ref, dot_nt)
    for copy in copies + [tok_copy]:
        copy.wait()


def front(seq_count, tokens, cotangent, weights, hashes):
    tok_rows, model_width = tokens.shape
    head_cols = weights[0].shape[1]
    outer, share = seq_count // 2, model_width // seq_count
    bits = seq_count.bit_length() - 1
    vmem = pl.BlockSpec(memory_space=pltpu.VMEM)
    hbm = pl.BlockSpec(memory_space=pl.ANY)
    dma = pltpu.SemaphoreType.DMA

    def array(*shape):
        return jax.ShapeDtypeStruct(shape, BF)

    cross_rows = sum(cross_rows_of(d) for d in range(1, seq_count))
    return pl.pallas_call(
        functools.partial(front_kernel, seq_count),
        in_specs=[hbm] * 6 + [vmem] * 4,
        out_specs=[vmem] * 11,
        out_shape=[array(*w.shape) for w in weights]
        + [array(tok_rows, head_cols)] * 4
        + [array(tok_rows // 2, 2 * head_cols), array(cross_rows, 2 * head_cols)]
        + [array(outer, tok_rows, share)],
        scratch_shapes=[
            pltpu.VMEM(tokens.shape, BF),
            pltpu.VMEM(tokens.shape, BF),
            pltpu.VMEM((3,) + weights[0].shape, BF),
            pltpu.VMEM(weights[3].shape, BF),
            pltpu.VMEM((model_width, LANES), jnp.int32),
            pltpu.VMEM((head_cols, LANES), jnp.int32),
            pltpu.VMEM((outer, tok_rows, share), BF),
            [pltpu.VMEM((tok_rows >> n + 2, 2 * head_cols), BF) for n in range(bits)],
            dma((6,)),
            dma((seq_count,)),
            dma((seq_count,)),
        ],
        compiler_params=pltpu.CompilerParams(
            collective_id=1, has_side_effects=True, vmem_limit_bytes=56 << 20
        ),
        cost_estimate=pl.CostEstimate(
            flops=8 * tok_rows * model_width * head_cols,
            bytes_accessed=32 << 20,
            transcendentals=0,
        ),
        name="front",
    )(tokens, cotangent, *weights, *hashes)


def tail_kernel(
    seq_count,
    head_count,
    q_ref,
    k_ref,
    v_ref,
    do_ref,
    kv1_ref,
    kvx_ref,
    upper_ref,
    tokens_ref,
    cot_ref,
    tok_pair_ref,
    wq_ref,
    wk_ref,
    wv_ref,
    wo_ref,
    attended_ref,
    grad_tok_ref,
    gq_ref,
    gk_ref,
    gv_ref,
    go_ref,
    att_ref,
    dq_ref,
    dk_own_ref,
    dv_own_ref,
    dkvx_ref,
    grads,
    pairs,
    tok_t,
    cot_t,
    tok_pair_t,
    half_out,
    half_in,
    back_in,
    head_out,
    head_in,
    chain_out,
    up_in,
    down_in,
    pair_send,
    pair_recv,
    dq_send,
    dq_recv,
    back_send,
    back_recv,
    head_send,
    head_recv,
    chain_send,
    up_recv,
    down_recv,
):
    seq_idx = lax.axis_index("seq")
    head_idx = lax.axis_index("head")
    outer = seq_count // 2
    z = seq_idx // 2
    inner = seq_idx % 2
    partner = flipped(seq_idx, 1)
    head_cols = att_ref.shape[1]

    outer_share = tok_pair_ref.shape[2]
    barrier = pltpu.get_barrier_semaphore()
    for apart in range(1, seq_count):
        greet("seq", flipped(seq_idx, apart))
    for apart in range(1, head_count):
        greet("head", (head_idx + apart) % head_count)
    pl.semaphore_wait(barrier, seq_count + head_count - 2)

    heads = head_cols // DH

    def head_columns(h, shift=0):
        return pl.ds(pl.multiple_of(h * DH + shift, DH), DH)

    def head_copies(h):
        cols = head_columns(h)
        copies = []
        at = 0
        for apart in range(1, seq_count):
            rows = pl.ds(at, cross_rows_of(apart))
            at += cross_rows_of(apart)
            copies.append(
                remote(
                    dkvx_ref.at[:, rows, cols],
                    back_in.at[:, rows, cols],
                    back_send.at[h, apart],
                    back_recv.at[h, apart],
                    "seq",
                    flipped(seq_idx, apart),
                )
            )
        copies.append(
            remote(
                dq_ref.at[:, cols],
                pairs.at[0, :, cols],
                dq_send.at[h],
                dq_recv.at[h],
                "seq",
                partner,
            )
        )
        return copies

    def one_head(h, carry):
        cols = head_columns(h)
        cross_cols = head_columns(h, head_cols)
        attend(
            q_ref.shape[0],
            kvx_ref.shape[0],
            q_ref.at[:, cols],
            k_ref.at[:, cols],
            v_ref.at[:, cols],
            do_ref.at[:, cols],
            kv1_ref.at[:, cols],
            kv1_ref.at[:, cross_cols],
            kvx_ref.at[:, cols],
            kvx_ref.at[:, cross_cols],
            att_ref.at[:, cols],
            dq_ref.at[:, cols],
            dk_own_ref.at[:, cols],
            dv_own_ref.at[:, cols],
            dkvx_ref.at[:, :, cols],
        )
        head_copies(h)[-1].start()
        return carry

    sources = (dq_ref, att_ref, grads.at[0], grads.at[1])
    outs = (gq_ref, go_ref, gk_ref, gv_ref)
    pair_copies = [None] + [
        remote(
            half_out if n == 1 else sources[n],
            half_in if n == 1 else pairs.at[n],
            pair_send.at[n],
            pair_recv.at[n],
            "seq",
            partner,
        )
        for n in range(1, 4)
    ]

    def transpose_into(dst, src):
        width = min(256, src.shape[1])

        def columns(i, carry):
            here = pl.ds(pl.multiple_of(i * width, width), width)
            dst[here, :] = src[:, here].astype(F32).T.astype(BF)
            return carry

        lax.fori_loop(0, src.shape[1] // width, columns, 0)

    def own_rows(n, which):
        return pl.ds(pl.multiple_of((2 * n + which) * outer_share, outer_share), outer_share)

    def send_terms(which, term, result_ref):
        copies = []
        for apart in range(1, head_count):
            peer = (head_idx + apart) % head_count
            head_out[which, apart - 1] = term(peer).astype(BF)
            copy = remote(
                head_out.at[which, apart - 1],
                head_in.at[which, apart - 1],
                head_send.at[which, apart - 1],
                head_recv.at[which, apart - 1],
                "head",
                peer,
            )
            copy.start()
            copies.append(copy)
        return copies

    def finish_terms(which, term, copies, result_ref):
        total = term(head_idx)
        for apart, copy in enumerate(copies):
            copy.wait()
            total = total + head_in[which, apart].astype(F32)
        result_ref[...] = total.astype(BF)

    def piece(n):
        return pl.ds(pl.multiple_of(n * head_cols, head_cols), head_cols)

    def out_term(n):
        return dot32(att_ref[...], wo_ref[:, piece(n)])

    def in_term(n):
        return (
            dot_nt(dq_ref[...], wq_ref[piece(n), :])
            + dot_nt(grads[0], wk_ref[piece(n), :])
            + dot_nt(grads[1], wv_ref[piece(n), :])
        )

    def partial(n, c):
        if n == 1:
            return dot32(cot_t[own_rows(c, inner), :], att_ref[...]) + half_in[c].astype(F32)
        mine = dot32(tok_t[own_rows(c, inner), :], sources[n][...])
        return mine + dot32(tok_pair_t[c], pairs[n])

    def up_copy(n, c):
        return remote(
            chain_out.at[n, c], up_in.at[n, c], chain_send.at[n, c], up_recv.at[n, c],
            "seq", (seq_idx + 2) % seq_count,
        )

    def down_copy(n, c):
        return remote(
            chain_out.at[n, c], down_in.at[n, c], chain_send.at[n, c], down_recv.at[n, c],
            "seq", (seq_idx + seq_count - 2) % seq_count,
        )

    def chain(n):
        if n > 0:
            pair_copies[n].wait_recv()

        def step(t, carry):
            @pl.when(z <= t - 1)
            def _():
                c = z + outer - t
                chain_out[n, c] = partial(n, c).astype(BF)

                @pl.when(z > 0)
                def _():
                    up_copy(n, c).wait_recv()
                    chain_out[n, c] = (
                        chain_out[n, c].astype(F32) + up_in[n, c].astype(F32)
                    ).astype(BF)

                up_copy(n, c).start()

            @pl.when(z >= outer - t)
            def _():
                c = z + t - outer
                chain_out[n, c] = partial(n, c).astype(BF)

                @pl.when(z < outer - 1)
                def _():
                    down_copy(n, c).wait_recv()
                    chain_out[n, c] = (
                        chain_out[n, c].astype(F32) + down_in[n, c].astype(F32)
                    ).astype(BF)

                down_copy(n, c).start()

            return carry

        lax.fori_loop(1, outer, step, 0)

    def finish_chain(n):
        own = partial(n, z)

        def store(total):
            outs[n][...] = total.T if n == 1 else total

        @pl.when(z == 0)
        def _():
            down_copy(n, z).wait_recv()
            store(own + down_in[n, z].astype(F32))

        @pl.when(z == outer - 1)
        def _():
            up_copy(n, z).wait_recv()
            store(own + up_in[n, z].astype(F32))

        @pl.when((z > 0) & (z < outer - 1))
        def _():
            up_copy(n, z).wait_recv()
            down_copy(n, z).wait_recv()
            store(own + up_in[n, z].astype(F32) + down_in[n, z].astype(F32))

    def send_back(h, carry):
        for copy in head_copies(h)[:-1]:
            copy.start()
        return carry

    lax.fori_loop(0, heads, one_head, 0)
    lax.fori_loop(0, heads, send_back, 0)
    transpose_into(tok_t, tokens_ref)

    def transpose_pair(c, carry):
        tok_pair_t[c] = tok_pair_ref[c].astype(F32).T.astype(BF)
        return carry

    lax.fori_loop(0, outer, transpose_pair, 0)

    def dq_arrived(h, carry):
        head_copies(h)[-1].wait_recv()
        return carry

    def back_arrived(h, carry):
        for copy in head_copies(h)[:-1]:
            copy.wait_recv()
        return carry

    lax.fori_loop(0, heads, dq_arrived, 0)

    @pl.when((z == 0) | (z == outer - 1))
    def _():
        chain(0)

    lax.fori_loop(0, heads, back_arrived, 0)
    grads[0] = (dk_own_ref[...] + dot32(upper_ref[...], back_in[0])).astype(BF)
    pair_copies[2].start()
    grads[1] = (dv_own_ref[...] + dot32(upper_ref[...], back_in[1])).astype(BF)
    pair_copies[3].start()

    @pl.when((z > 0) & (z < outer - 1))
    def _():
        chain(0)

    att_copies = send_terms(0, out_term, attended_ref)
    transpose_into(cot_t, cot_ref)

    def send_half(c, carry):
        half_out[c] = dot32(cot_t[own_rows(c, 1 - inner), :], att_ref[...]).astype(BF)
        return carry

    lax.fori_loop(0, outer, send_half, 0)
    pair_copies[1].start()
    tok_copies = send_terms(1, in_term, grad_tok_ref)
    chain(2)
    finish_chain(0)
    chain(3)
    finish_terms(0, out_term, att_copies, attended_ref)
    finish_chain(2)
    chain(1)
    finish_terms(1, in_term, tok_copies, grad_tok_ref)
    finish_chain(3)
    finish_chain(1)
    for copy in pair_copies[1:]:
        copy.wait_send()

    def head_sent(h, carry):
        for copy in head_copies(h):
            copy.wait_send()
        return carry

    lax.fori_loop(0, heads, head_sent, 0)

    def drain(c, carry):
        @pl.when(c != z)
        def _():
            for n in range(4):
                up_copy(n, c).wait_send()

        return carry

    lax.fori_loop(0, outer, drain, 0)


def tail(seq_count, head_count, *arrays):
    queries, kvx, tokens, tok_pair = arrays[0], arrays[5], arrays[7], arrays[9]
    tok_rows, head_cols = queries.shape
    cross = (2, kvx.shape[0], head_cols)
    heads = head_cols // DH
    outer, _, share = tok_pair.shape
    vmem = pl.BlockSpec(memory_space=pltpu.VMEM)
    chunk = (4, outer, share, head_cols)
    grad = jax.ShapeDtypeStruct((share, head_cols), F32)
    tokens_out = jax.ShapeDtypeStruct((tok_rows, head_cols), BF)
    dma = pltpu.SemaphoreType.DMA
    return pl.pallas_call(
        functools.partial(tail_kernel, seq_count, head_count),
        in_specs=[vmem] * len(arrays),
        out_specs=[vmem] * 6,
        out_shape=[tokens_out] * 2
        + [grad] * 3
        + [jax.ShapeDtypeStruct((head_cols, share), F32)],
        scratch_shapes=[
            pltpu.VMEM((tok_rows, head_cols), BF),
            pltpu.VMEM((tok_rows, head_cols), BF),
            pltpu.VMEM((tok_rows, head_cols), F32),
            pltpu.VMEM((tok_rows, head_cols), F32),
            pltpu.VMEM(cross, BF),
            pltpu.VMEM((2, tok_rows, head_cols), BF),
            pltpu.VMEM((4, tok_rows, head_cols), BF),
            pltpu.VMEM(tokens.shape[::-1], BF),
            pltpu.VMEM(tokens.shape[::-1], BF),
            pltpu.VMEM((outer, share, tok_rows), BF),
            pltpu.VMEM((outer, share, head_cols), BF),
            pltpu.VMEM((outer, share, head_cols), BF),
            pltpu.VMEM(cross, BF),
            pltpu.VMEM((2, head_count - 1, tok_rows, head_cols), BF),
            pltpu.VMEM((2, head_count - 1, tok_rows, head_cols), BF),
            pltpu.VMEM(chunk, BF),
            pltpu.VMEM(chunk, BF),
            pltpu.VMEM(chunk, BF),
            dma((4,)),
            dma((4,)),
            dma((heads,)),
            dma((heads,)),
            dma((heads, seq_count)),
            dma((heads, seq_count)),
            dma((2, head_count - 1)),
            dma((2, head_count - 1)),
            dma((4, outer)),
            dma((4, outer)),
            dma((4, outer)),
        ],
        compiler_params=pltpu.CompilerParams(
            collective_id=0, has_side_effects=True, vmem_limit_bytes=60 << 20
        ),
        cost_estimate=pl.CostEstimate(
            flops=20 * tok_rows * head_cols * share * outer,
            bytes_accessed=32 << 20,
            transcendentals=0,
        ),
        name="tail",
    )(*arrays)


def settle_kernel(*refs):
    count = len(refs) // 2
    for n in range(count):
        refs[count + n][...] = refs[n][...]


def settle(arrays):
    steps = 4
    specs = [pl.BlockSpec((a.shape[0] // steps, a.shape[1]), lambda i: (i, 0)) for a in arrays]
    return pl.pallas_call(
        settle_kernel,
        grid=(steps,),
        in_specs=specs,
        out_specs=specs,
        out_shape=[jax.ShapeDtypeStruct(a.shape, a.dtype) for a in arrays],
        name="settle",
    )(*arrays)


def body(tokens, cotangent, w_query, w_key, w_value, w_out, seeds):
    seq_count = lax.axis_size("seq")
    head_count = lax.axis_size("head")
    head_idx = lax.axis_index("head")
    tok_rows, model_width = tokens.shape
    head_cols = w_query.shape[1]
    all_ids = jnp.arange(model_width, dtype=jnp.int32)
    own_ids = head_idx * head_cols + jnp.arange(head_cols, dtype=jnp.int32)

    def hash_cols(ids, seed):
        seeded = (ids * 10007 % prime_mod + seed * 31337 % prime_mod) % prime_mod
        return centre(seeded)[None, :]

    hashes = [hash_cols(own_ids, seeds[n]) for n in range(3)] + [hash_cols(all_ids, seeds[3])]
    (
        query_w,
        key_w,
        value_w,
        out_w,
        queries,
        keys,
        values,
        grad_att,
        kv1,
        kvx,
        tok_pair,
    ) = front(seq_count, tokens, cotangent, (w_query, w_key, w_value, w_out), hashes)
    return tuple(
        settle(
            tail(
                seq_count,
                head_count,
                queries,
                keys,
                values,
                grad_att,
                kv1,
                kvx,
                upper_matrix(tok_rows, seq_count),
                tokens,
                cotangent,
                tok_pair,
                query_w,
                key_w,
                value_w,
                out_w,
            )
        )
    )


def solution(mesh):
    in_specs = (
        P("seq", None),
        P("seq", None),
        P(None, "head"),
        P(None, "head"),
        P(None, "head"),
        P("head", None),
        P(),
    )
    out_specs = (
        P("seq", "head"),
        P("seq", "head"),
        P("seq", "head"),
        P("seq", "head"),
        P("seq", "head"),
        P("head", "seq"),
    )
    return jax.shard_map(body, mesh=mesh, in_specs=in_specs, out_specs=out_specs, check_vma=False)
```
